256 devices in a mesh: blk: 16 (over y_lo, z), grp: 16 (over y_hi, x, core).
Axes of the slice: x: 4, y: 4 (y_hi: 2, y_lo: 2; y = y_hi * 2 + y_lo), z: 8, core: 2. Of those that a mesh axis runs over, the one named last changes fastest.
Arguments:
- queries: bfloat16 [20, 32768, 128], P(None, ('blk', 'grp')), may hold values from -125 to 125
- keys: bfloat16 [20, 32768, 128], P(None, ('blk', 'grp')), may hold values from -6 to 6
- values: bfloat16 [20, 32768, 128], P(None, ('blk', 'grp')), may hold values from -6 to 6
- tile_cluster: int32 [20, 256], P(None, ('blk', 'grp')), may hold values from 0 to 255, as said below
Outputs:
- attended: bfloat16 [20, 32768, 128], P(None, ('blk', 'grp'))
The draws below stay inside these ranges and needn't reach their ends.
Inputs may be any that keep to these rules, and one draw needn't show every extreme that they name: `tile_cluster`: cluster c is served by grp index c % 16. In each group of 16 consecutive tiles (one blk index), over all heads, every server has exactly 20 tiles, at most 2 of them at one tile index; the tiles of one head with one cluster in one group are exactly 4 or none. Cluster numbers are uneven: low ones are far more common.
All inputs are finite; a program needn't handle non-finite values.
Results may differ from the reference program's by a relative error of at most 0.0038.
Values may be sent and summed in bfloat16 or wider, within the bound.
No kernel may reach another device: no remote copies, remote signals or barrier semaphores. Data moves between devices by JAX's collectives and lax.ppermute only.
A program may use at most 128 MiB of HBM per device.

```python
import jax
import jax.numpy as jnp
from jax import lax

HEADS = 20
HEAD_SIZE = 128
TILE = 128
MATCH = 4
TILES = 256
TOKENS = 32768
OWNED = 16
N_BLK = 16
N_GRP = 16


def base_keys(key):
    return jax.random.truncated_normal(key, -6.0, 6.0, (HEADS, TOKENS, HEAD_SIZE), jnp.float32)


def draw_keys(key, part):
    shared = base_keys(key)
    return shared.astype(jnp.bfloat16)


def draw_queries(key, part):
    key = jax.random.fold_in(key, 11)
    fresh = jax.random.truncated_normal(key, -6.0, 6.0, (HEADS, TOKENS, HEAD_SIZE), jnp.float32)
    return fresh.astype(jnp.bfloat16)


def draw_tile_cluster(key, part):
    key = jax.random.fold_in(key, 7)
    order_key, shift_key, first_key, second_key = jax.random.split(key, 4)
    order = jax.random.permutation(order_key, HEADS).astype(jnp.int32)
    shift = jax.random.randint(shift_key, (), 0, N_GRP, dtype=jnp.int32)
    tile_ids = jnp.arange(TILES, dtype=jnp.int32)
    device_block = tile_ids % N_GRP // MATCH
    server = (order[:, None] + device_block[None, :] * MATCH + shift) % N_GRP
    blocks_per_group = N_GRP // MATCH
    unit_index = tile_ids // N_GRP * blocks_per_group + device_block
    unit_total = N_BLK * blocks_per_group
    first_pick = jax.random.randint(first_key, (HEADS, unit_total), 0, OWNED, dtype=jnp.int32)
    second_pick = jax.random.randint(second_key, (HEADS, unit_total), 0, OWNED, dtype=jnp.int32)
    picked = first_pick * second_pick // OWNED
    unit_group = (jnp.arange(unit_total, dtype=jnp.int32) // blocks_per_group)[None, :]
    picked = jnp.where(unit_group == 0, OWNED - 1, jnp.where(unit_group == N_BLK - 1, 0, picked)).astype(jnp.int32)
    rank_in_server = jnp.take(picked, unit_index, axis=1)
    return (server + N_GRP * rank_in_server).astype(jnp.int32)


def shard_levels(key, dims, pieces, least, largest):
    def one(dim, parts):
        heights = jax.random.uniform(jax.random.fold_in(jax.random.fold_in(key, 6), dim), (parts,), jnp.float32, least / len(pieces), largest / len(pieces))
        return jnp.repeat(jnp.exp(heights), dims[dim] // parts).reshape((-1,) + (1,) * (len(dims) - dim - 1))

    loudness = one(*pieces[0])
    for cut in pieces[1:]:
        loudness = loudness * one(*cut)
    return loudness


def centred(key, dims, deviation, bound, pieces=(), held_as=jnp.bfloat16):
    result = jax.random.normal(key, dims, jnp.float32) * deviation
    if len(pieces) > 0:
        result = shard_levels(key, dims, pieces, -0.22, 0.18) * result
    return jnp.clip(result, min=-bound, max=bound).astype(held_as)


def setup_inputs(seed: int = 0) -> dict:
    key_list = jax.random.split(jax.random.key(seed), 5)
    queries = draw_queries(jax.random.fold_in(key_list[4], 71), 0)
    keys = draw_keys(jax.random.fold_in(key_list[4], 71), 0)
    values = centred(key_list[2], (HEADS, TOKENS, HEAD_SIZE), 1.0, 6.0, ((1, 256),))
    tile_cluster = draw_tile_cluster(jax.random.fold_in(key_list[4], 71), 0)
    return {"queries": queries, "keys": keys, "values": values, "tile_cluster": tile_cluster}


NEGATIVE = -1e30


def reference(queries, keys, values, tile_cluster):
    tile_count = TOKENS // TILE
    reach = MATCH * N_BLK
    query_tiles = queries.reshape(HEADS, tile_count, TILE, HEAD_SIZE)
    key_tiles = keys.reshape(HEADS, tile_count, TILE, HEAD_SIZE)
    value_tiles = values.reshape(HEADS, tile_count, TILE, HEAD_SIZE)
    tile_ids = jnp.arange(tile_count, dtype=jnp.int32)
    offsets = jnp.arange(TILE, dtype=jnp.int32)
    score_scale = HEAD_SIZE ** -0.5

    def pick_tiles(tiles, picks):
        return jnp.take(tiles, picks, axis=0)

    def one_tile(index):
        here = lax.dynamic_slice_in_dim(tile_cluster, index, 1, 1)
        matched = (tile_cluster == here) & (tile_ids[None, :] <= index)
        priority = jnp.where(matched, tile_count - tile_ids[None, :], 0).astype(jnp.int32)
        top_values, top_index = lax.top_k(priority, reach)
        top_index = top_index.astype(jnp.int32)
        chosen_keys = jax.vmap(pick_tiles)(key_tiles, top_index)
        chosen_values = jax.vmap(pick_tiles)(value_tiles, top_index)
        query_rows = lax.dynamic_index_in_dim(query_tiles, index, 1, keepdims=False)
        scores = jnp.einsum("hqd,hmkd->hqmk", query_rows.astype(jnp.float32), chosen_keys.astype(jnp.float32)) * score_scale
        key_position = top_index[:, :, None] * TILE + offsets
        query_position = index * TILE + offsets
        visible = (top_values > 0)[:, None, :, None] & (key_position[:, None, :, :] <= query_position[None, :, None, None])
        peak = jnp.max(jnp.where(visible, scores, NEGATIVE), axis=(2, 3))
        raw = jnp.where(visible, jnp.exp(scores - peak[:, :, None, None]), 0.0)
        total = jnp.sum(raw, axis=(2, 3))
        weights = lax.optimization_barrier(raw.astype(jnp.bfloat16))
        mixed = jnp.einsum("hqmk,hmkd->hqd", weights.astype(jnp.float32), chosen_values.astype(jnp.float32))
        return (mixed / total[:, :, None]).astype(jnp.bfloat16)

    stacked = lax.map(one_tile, tile_ids)
    return jnp.transpose(stacked, (1, 0, 2, 3)).reshape(HEADS, TOKENS, HEAD_SIZE)
```

```python
from functools import partial

import jax
import jax.numpy as jnp
from jax import lax
from jax.experimental import pallas as pl
from jax.experimental.pallas import tpu as pltpu
from jax.sharding import Mesh
from jax.sharding import PartitionSpec as P

AXES = ("ylo", "z", "yhi", "x", "core")
PLANE = ("ylo", "yhi", "x", "core")
SIZES = (2, 8, 2, 4, 2)

HEADS = 20
PLANES = 8
PER_PLANE = 3
SLOT_HEADS = PLANES * PER_PLANE
SERVERS = 32
GROUPS = 16
GROUP_TILES = 16
TILES = 256
TILE = 128
MATCH = 4
UNITS = PER_PLANE * GROUPS * GROUP_TILES // MATCH
PIECE = TILE // SERVERS
HEAD_SIZE = 128
LIMIT = 16
CAPACITIES = (8, 9, 10, 12, 16)
ROWS = MATCH * TILE
UNIT_PIECE = MATCH * PIECE
NEGATIVE = -1e30
VMEM = 56 * 1024 * 1024


def assign_kernel(count_ref, size_ref, key_ref, load_ref):
    lane = lax.broadcasted_iota(jnp.int32, (PLANES, 128), 1)
    load_ref[...] = jnp.where(lane < SERVERS, 0.0, 1e6)

    def step(i, carry):
        load = load_ref[...]
        key = jnp.min(load * 128.0 + lane.astype(jnp.float32), axis=1, keepdims=True)
        best = jnp.floor(key * (1.0 / 128.0))
        owner = (key - best * 128.0).astype(jnp.int32)
        load_ref[...] = load + jnp.where(lane == owner, size_ref[i], 0.0)
        key_ref[i] = jnp.broadcast_to(key, (PLANES, 128)).astype(jnp.int32)
        return carry

    lax.fori_loop(0, count_ref[0], step, 0)


def assign(count, sizes):
    return pl.pallas_call(
        assign_kernel,
        in_specs=[
            pl.BlockSpec(memory_space=pltpu.SMEM),
            pl.BlockSpec(memory_space=pltpu.VMEM),
        ],
        out_specs=[pl.BlockSpec(memory_space=pltpu.VMEM)] * 2,
        out_shape=[
            jax.ShapeDtypeStruct((UNITS, PLANES, 128), jnp.int32),
            jax.ShapeDtypeStruct((PLANES, 128), jnp.float32),
        ],
        compiler_params=pltpu.CompilerParams(vmem_limit_bytes=VMEM),
        name="assign",
    )(count, sizes)


def pack_kernel(capacity, count_ref, tile_ref, place_ref, in_ref, out_ref):
    def unit(i, carry):
        code = place_ref[i]
        slot = (code // LIMIT) * capacity + lax.rem(code, LIMIT)
        head = i // (UNITS // PER_PLANE)
        for j in range(MATCH):
            tile = tile_ref[i * MATCH + j]
            for s in range(3):
                out_ref[slot, s, j] = in_ref[tile, head * 3 + s]
        return carry

    lax.fori_loop(0, count_ref[0], unit, 0)


def pack(capacity, count, tiles, place, arrived):
    smem = pl.BlockSpec(memory_space=pltpu.SMEM)
    vmem = pl.BlockSpec(memory_space=pltpu.VMEM)
    return pl.pallas_call(
        partial(pack_kernel, capacity),
        in_specs=[smem, smem, smem, vmem],
        out_specs=vmem,
        out_shape=jax.ShapeDtypeStruct(
            (SERVERS * capacity, 3, MATCH, PIECE, HEAD_SIZE), jnp.bfloat16
        ),
        compiler_params=pltpu.CompilerParams(vmem_limit_bytes=VMEM),
        name="pack_units",
    )(count, tiles, place, arrived)


def unpack_kernel(capacity, count_ref, tile_ref, place_ref, in_ref, out_ref):
    def unit(i, carry):
        code = place_ref[i]
        slot = (code // LIMIT) * capacity + lax.rem(code, LIMIT)
        head = i // (UNITS // PER_PLANE)
        for j in range(MATCH):
            tile = tile_ref[i * MATCH + j]
            out_ref[tile, head] = in_ref[slot, j]
        return carry

    lax.fori_loop(0, count_ref[0], unit, 0)


def unpack(capacity, count, tiles, place, results):
    smem = pl.BlockSpec(memory_space=pltpu.SMEM)
    vmem = pl.BlockSpec(memory_space=pltpu.VMEM)
    return pl.pallas_call(
        partial(unpack_kernel, capacity),
        in_specs=[smem, smem, smem, vmem],
        out_specs=vmem,
        out_shape=jax.ShapeDtypeStruct((TILES, PER_PLANE, PIECE, HEAD_SIZE), jnp.bfloat16),
        compiler_params=pltpu.CompilerParams(vmem_limit_bytes=VMEM),
        name="unpack_units",
    )(count, tiles, place, results)


def row_key(shape, dim):
    row = lax.broadcasted_iota(jnp.int32, shape, dim)
    piece = row // UNIT_PIECE
    tile = lax.rem(row // PIECE, MATCH)
    return tile * TILE + piece * PIECE + lax.rem(row, PIECE)


def attend_kernel(used_ref, rank_ref, in_ref, out_ref, peak_ref, total_ref, sum_ref):
    factor = HEAD_SIZE**-0.5 * 1.4426950408889634

    def rows(unit, which):
        return in_ref[:, unit, which].reshape(ROWS, HEAD_SIZE)

    def scores_of(query, unit):
        return lax.dot_general(
            query, rows(unit, 1), (((1,), (1,)), ((), ())), preferred_element_type=jnp.float32
        )

    def one_query_unit(unit, carry):
        query = rows(unit, 0)
        scores = scores_of(query, unit)
        visible = row_key((1, ROWS), 1) <= row_key((ROWS, 1), 0)
        scores = jnp.where(visible, scores, NEGATIVE)
        peak = jnp.max(scores, axis=1, keepdims=True)
        weights = jnp.exp2((scores - peak) * factor)
        peak_ref[...] = peak
        total_ref[...] = jnp.sum(weights, axis=1, keepdims=True)
        sum_ref[...] = jnp.dot(
            weights.astype(jnp.bfloat16), rows(unit, 2), preferred_element_type=jnp.float32
        )

        def earlier(other, carry):
            scores = scores_of(query, other)
            old = peak_ref[...]
            peak = jnp.maximum(old, jnp.max(scores, axis=1, keepdims=True))
            weights = jnp.exp2((scores - peak) * factor)
            keep = jnp.exp2((old - peak) * factor)
            peak_ref[...] = peak
            total_ref[...] = total_ref[...] * keep + jnp.sum(weights, axis=1, keepdims=True)
            sum_ref[...] = sum_ref[...] * keep + jnp.dot(
                weights.astype(jnp.bfloat16), rows(other, 2), preferred_element_type=jnp.float32
            )
            return carry

        lax.fori_loop(unit - rank_ref[unit], unit, earlier, 0)
        result = (sum_ref[...] / total_ref[...]).astype(jnp.bfloat16)
        out_ref[:, unit] = result.reshape(SERVERS, UNIT_PIECE, HEAD_SIZE)
        return carry

    lax.fori_loop(0, used_ref[0], one_query_unit, 0)


def attend(capacity, used, ranks, units):
    smem = pl.BlockSpec(memory_space=pltpu.SMEM)
    vmem = pl.BlockSpec(memory_space=pltpu.VMEM)
    return pl.pallas_call(
        attend_kernel,
        in_specs=[smem, smem, vmem],
        out_specs=vmem,
        out_shape=jax.ShapeDtypeStruct(
            (SERVERS, capacity, UNIT_PIECE, HEAD_SIZE), jnp.bfloat16
        ),
        scratch_shapes=[
            pltpu.VMEM((ROWS, 1), jnp.float32),
            pltpu.VMEM((ROWS, 1), jnp.float32),
            pltpu.VMEM((ROWS, HEAD_SIZE), jnp.float32),
        ],
        compiler_params=pltpu.CompilerParams(vmem_limit_bytes=VMEM),
        name="attend",
    )(used, ranks, units)


def plan(clusters):
    plane = lax.axis_index("z")
    server = lax.axis_index(PLANE)
    clusters = jnp.pad(clusters.T, ((0, SLOT_HEADS - HEADS), (0, 0)))
    tiles = clusters.reshape(SLOT_HEADS, GROUPS, GROUP_TILES)
    index = jnp.arange(GROUP_TILES, dtype=jnp.int32)
    mine, other = tiles[:, :, :, None], tiles[:, :, None, :]
    ahead = (other < mine) | ((other == mine) & (index[None, :] < index[:, None]))
    place = jnp.sum(ahead, axis=3, dtype=jnp.int32)
    at_place = place[:, :, None, :] == index[:, None]
    unit_cluster = jnp.sum(
        jnp.where(at_place[:, :, ::MATCH], tiles[:, :, None, :], 0), axis=3
    ).reshape(SLOT_HEADS, -1)
    units = unit_cluster.shape[1]
    number = jnp.arange(units, dtype=jnp.int32)
    same = unit_cluster[:, :, None] == unit_cluster[:, None, :]
    size = jnp.sum(same, axis=2, dtype=jnp.int32)
    rank = jnp.sum(same & (number[None, :] < number[:, None]), axis=2, dtype=jnp.int32)
    real = jnp.arange(SLOT_HEADS)[:, None] < HEADS
    lead = jnp.where((rank == 0) & real, size, 0).reshape(PLANES, UNITS)
    every = jnp.arange(UNITS, dtype=jnp.int32)
    mine, other = lead[:, :, None], lead[:, None, :]
    order = jnp.sum(
        (other > mine) | ((other == mine) & (every[None, :] < every[:, None])),
        axis=2,
        dtype=jnp.int32,
    )
    sizes = jnp.sum(
        jnp.where(order[:, None, :] == every[:, None], lead[:, None, :], 0), axis=2
    )
    count = jnp.max(jnp.sum(lead > 0, axis=1, dtype=jnp.int32)).reshape(1)
    sizes = jnp.broadcast_to(
        sizes.T.astype(jnp.float32)[:, :, None], (UNITS, PLANES, 128)
    )
    key, load = assign(count, sizes)
    load = jnp.where(jnp.arange(128)[None, :] < SERVERS, load, 0.0).astype(jnp.int32)
    most = jnp.max(load)
    key = lax.dynamic_index_in_dim(key[:, :, 0], plane, 1, keepdims=False)
    load = lax.dynamic_index_in_dim(load, plane, 0, keepdims=False)
    first = plane * PER_PLANE

    def own(array):
        return lax.dynamic_slice_in_dim(array, first, PER_PLANE, 0)

    own_order = lax.dynamic_index_in_dim(order, plane, 0, keepdims=False)
    own_order = own_order.reshape(PER_PLANE, 1, units)
    own_same, own_rank = own(same), own(rank)
    item = jnp.sum(
        jnp.where(own_same & (own_rank == 0)[:, None, :], own_order, 0), axis=2
    ).reshape(UNITS)
    code = jnp.sum(jnp.where(item[:, None] == every[None, :], key[None, :], 0), axis=1)
    own_rank = own_rank.reshape(UNITS)
    owner, slot = code % 128, code // 128 + own_rank
    own_count = jnp.clip(HEADS - first, 0, PER_PLANE) * units
    live = every < own_count
    tile_of = own(
        jnp.sum(
            jnp.where(at_place, index, 0), axis=3, dtype=jnp.int32
        )
    ) + jnp.arange(GROUPS, dtype=jnp.int32)[:, None] * GROUP_TILES
    here = (owner == server)[None, :] & live[None, :] & (
        slot[None, :] == jnp.arange(LIMIT, dtype=jnp.int32)[:, None]
    )
    ranks = jnp.sum(jnp.where(here, own_rank[None, :], 0), axis=1)
    used = jnp.sum(jnp.where(jnp.arange(128) == server, load, 0)).reshape(1)
    return own_count.reshape(1), tile_of.reshape(-1), owner * LIMIT + slot, ranks, used, most


def exchange(capacity, arrived, count, tiles, place, ranks, used):
    packed = pack(capacity, count, tiles, place, arrived)
    packed = packed.reshape(SERVERS, capacity, 3, UNIT_PIECE, HEAD_SIZE)
    units = lax.all_to_all(packed, PLANE, split_axis=0, concat_axis=0, tiled=True)
    results = attend(capacity, used, ranks, units)
    results = lax.all_to_all(results, PLANE, split_axis=0, concat_axis=0, tiled=True)
    results = results.reshape(SERVERS * capacity, MATCH, PIECE, HEAD_SIZE)
    return unpack(capacity, count, tiles, place, results)


def on_device(queries, keys, values, tile_cluster):
    clusters = jnp.broadcast_to(tile_cluster.reshape(1, HEADS), (TILES, HEADS))
    clusters = lax.all_to_all(clusters, AXES, split_axis=0, concat_axis=0, tiled=True)
    stacked = jnp.stack([queries, keys, values], axis=1)
    stacked = jnp.pad(stacked, ((0, SLOT_HEADS - HEADS), (0, 0), (0, 0), (0, 0)))
    stacked = stacked.reshape(PLANES, PER_PLANE, 3, 2, SERVERS // 2, PIECE, HEAD_SIZE)
    outgoing = stacked.transpose(3, 0, 4, 1, 2, 5, 6)
    outgoing = outgoing.reshape(TILES, PER_PLANE * 3, PIECE, HEAD_SIZE)
    arrived = lax.all_to_all(outgoing, AXES, split_axis=0, concat_axis=0, tiled=True)
    count, tiles, place, ranks, used, most = plan(clusters)
    which = sum((most > capacity).astype(jnp.int32) for capacity in CAPACITIES[:-1])
    back = lax.switch(
        which,
        [partial(exchange, capacity) for capacity in CAPACITIES],
        arrived,
        count,
        tiles,
        place,
        ranks,
        used,
    )
    back = lax.all_to_all(back, AXES, split_axis=0, concat_axis=0, tiled=True)
    back = back.reshape(2, PLANES, SERVERS // 2, PER_PLANE, PIECE, HEAD_SIZE)
    back = back.transpose(1, 3, 0, 2, 4, 5).reshape(SLOT_HEADS, TILE, HEAD_SIZE)
    return back[:HEADS]


def solution(mesh):
    fine = Mesh(mesh.devices.reshape(SIZES), AXES)
    rows = ("ylo", "z", "yhi", "x", "core")
    return jax.shard_map(
        on_device,
        mesh=fine,
        in_specs=(
            P(None, rows, None),
            P(None, rows, None),
            P(None, rows, None),
            P(None, rows),
        ),
        out_specs=P(None, rows, None),
        check_vma=False,
    )
```

```python
from functools import partial

import jax
import jax.numpy as jnp
from jax import lax
from jax.experimental import pallas as pl
from jax.experimental.pallas import tpu as pltpu
from jax.sharding import Mesh
from jax.sharding import PartitionSpec as P

AXES = ("ylo", "z", "yhi", "x", "core")
PLANE = ("ylo", "yhi", "x", "core")
SIZES = (2, 8, 2, 4, 2)

HEADS = 20
PLANES = 8
PER_PLANE = 3
SLOT_HEADS = PLANES * PER_PLANE
SERVERS = 32
GROUPS = 16
GROUP_TILES = 16
TILES = 256
TILE = 128
MATCH = 4
UNITS = PER_PLANE * GROUPS * GROUP_TILES // MATCH
PIECE = TILE // SERVERS
HEAD_SIZE = 128
LIMIT = 16
CAPACITIES = ((8, 7), (9, 7), (10, 7), (11, 8), (13, 10), (16, 16))
SPLIT = 7
SCALE = 32
STEP = 4
ROWS = MATCH * TILE
UNIT_PIECE = MATCH * PIECE
NEGATIVE = -1e30
VMEM = 56 * 1024 * 1024


def assign_kernel(count_ref, size_ref, key_ref, load_ref):
    lane = lax.broadcasted_iota(jnp.int32, (PLANES, 128), 1)
    lane_number = lane.astype(jnp.float32)
    load_ref[...] = jnp.where(lane < SERVERS, 0.0, 65536.0)

    def step(i, carry):
        load = load_ref[...]
        key = jnp.min(load * 128.0 + lane_number, axis=1, keepdims=True)
        owner = key - jnp.floor(key * (1.0 / 128.0)) * 128.0
        load_ref[...] = load + jnp.where(lane_number == owner, size_ref[i], 0.0)
        key_ref[i] = jnp.broadcast_to(key, (PLANES, 128))
        return carry

    lax.fori_loop(0, count_ref[0], step, 0)


def assign(count, sizes):
    return pl.pallas_call(
        assign_kernel,
        in_specs=[
            pl.BlockSpec(memory_space=pltpu.SMEM),
            pl.BlockSpec(memory_space=pltpu.VMEM),
        ],
        out_specs=[pl.BlockSpec(memory_space=pltpu.VMEM)] * 2,
        out_shape=[
            jax.ShapeDtypeStruct((UNITS, PLANES, 128), jnp.float32),
            jax.ShapeDtypeStruct((PLANES, 128), jnp.float32),
        ],
        compiler_params=pltpu.CompilerParams(vmem_limit_bytes=VMEM),
        name="assign",
    )(count, sizes)


def slab(code, depth, start, width):
    return (code // SCALE) * depth + start + lax.rem(code, SCALE) * width


def pack_kernel(caps, count_ref, tile_ref, place_ref, in_ref, out_ref):
    key_units, query_units = caps
    depth = 2 * key_units + query_units

    def unit(i):
        head = i // (UNITS // PER_PLANE)
        tiles = [tile_ref[i * MATCH + j] for j in range(MATCH)]
        to_query = slab(place_ref[i], depth, 2 * key_units, 1)
        to_keys = slab(place_ref[UNITS + i], depth, 0, 2)
        second = place_ref[2 * UNITS + i]
        for j in range(MATCH):
            out_ref[to_query, j] = in_ref[tiles[j], head * 3]
            out_ref[to_keys, j] = in_ref[tiles[j], head * 3 + 1]
            out_ref[to_keys + 1, j] = in_ref[tiles[j], head * 3 + 2]

        @pl.when(second >= 0)
        def _():
            also = slab(second, depth, 0, 2)
            for j in range(MATCH):
                out_ref[also, j] = in_ref[tiles[j], head * 3 + 1]
                out_ref[also + 1, j] = in_ref[tiles[j], head * 3 + 2]

    def some(i, carry):
        for k in range(STEP):
            unit(i * STEP + k)
        return carry

    lax.fori_loop(0, count_ref[0] // STEP, some, 0)


def pack(caps, count, tiles, place, arrived):
    smem = pl.BlockSpec(memory_space=pltpu.SMEM)
    vmem = pl.BlockSpec(memory_space=pltpu.VMEM)
    return pl.pallas_call(
        partial(pack_kernel, caps),
        in_specs=[smem, smem, smem, vmem],
        out_specs=vmem,
        out_shape=jax.ShapeDtypeStruct(
            (SERVERS * (2 * caps[0] + caps[1]), MATCH, PIECE, HEAD_SIZE), jnp.bfloat16
        ),
        compiler_params=pltpu.CompilerParams(vmem_limit_bytes=VMEM),
        name="pack_units",
    )(count, tiles, place, arrived)


def unpack_kernel(caps, count_ref, tile_ref, place_ref, in_ref, out_ref):
    def some(i, carry):
        for k in range(STEP):
            unit = i * STEP + k
            slot = slab(place_ref[unit], caps[1], 0, 1)
            head = unit // (UNITS // PER_PLANE)
            for j in range(MATCH):
                out_ref[tile_ref[unit * MATCH + j], head] = in_ref[slot, j]
        return carry

    lax.fori_loop(0, count_ref[0] // STEP, some, 0)


def unpack(caps, count, tiles, place, results):
    smem = pl.BlockSpec(memory_space=pltpu.SMEM)
    vmem = pl.BlockSpec(memory_space=pltpu.VMEM)
    return pl.pallas_call(
        partial(unpack_kernel, caps),
        in_specs=[smem, smem, smem, vmem],
        out_specs=vmem,
        out_shape=jax.ShapeDtypeStruct((TILES, PER_PLANE, PIECE, HEAD_SIZE), jnp.bfloat16),
        compiler_params=pltpu.CompilerParams(vmem_limit_bytes=VMEM),
        name="unpack_units",
    )(count, tiles, place, results)


def row_key(shape, dim):
    row = lax.broadcasted_iota(jnp.int32, shape, dim)
    piece = row // UNIT_PIECE
    tile = lax.rem(row // PIECE, MATCH)
    return tile * TILE + piece * PIECE + lax.rem(row, PIECE)


def attend_kernel(caps, used_ref, table_ref, in_ref, out_ref, peak_ref, total_ref, sum_ref, turned_ref):
    factor = HEAD_SIZE**-0.5 * 1.4426950408889634

    def rows(which):
        return in_ref[:, which].reshape(ROWS, HEAD_SIZE)

    def turn(unit, carry):
        turned_ref[unit] = rows(2 * unit + 1).T
        return carry

    lax.fori_loop(0, used_ref[1], turn, 0)

    def one_query_unit(slot, carry):
        code = table_ref[slot]
        first = code // SCALE
        last = first + lax.rem(code, SCALE)
        query = rows(2 * caps[0] + slot)

        def scores_of(unit):
            return lax.dot_general(
                rows(2 * unit), query, (((1,), (1,)), ((), ())), preferred_element_type=jnp.float32
            )

        def weigh(unit, weights):
            return jnp.dot(
                turned_ref[unit], weights.astype(jnp.bfloat16), preferred_element_type=jnp.float32
            )

        visible = row_key((ROWS, 1), 0) <= row_key((1, ROWS), 1)
        scores = jnp.where(visible, scores_of(last), NEGATIVE)
        peak = jnp.max(scores, axis=0, keepdims=True)
        weights = jnp.exp2((scores - peak) * factor)
        peak_ref[...] = peak
        total_ref[...] = jnp.sum(weights, axis=0, keepdims=True)
        sum_ref[...] = weigh(last, weights)

        def earlier(unit, carry):
            scores = scores_of(unit)
            old = peak_ref[...]
            peak = jnp.maximum(old, jnp.max(scores, axis=0, keepdims=True))
            weights = jnp.exp2((scores - peak) * factor)
            keep = jnp.exp2((old - peak) * factor)
            peak_ref[...] = peak
            total_ref[...] = total_ref[...] * keep + jnp.sum(weights, axis=0, keepdims=True)
            sum_ref[...] = sum_ref[...] * keep + weigh(unit, weights)
            return carry

        lax.fori_loop(first, last, earlier, 0)
        result = (sum_ref[...] / total_ref[...]).T.astype(jnp.bfloat16)
        out_ref[:, slot] = result.reshape(SERVERS, UNIT_PIECE, HEAD_SIZE)
        return carry

    lax.fori_loop(0, used_ref[0], one_query_unit, 0)


def attend(caps, used, table, units):
    smem = pl.BlockSpec(memory_space=pltpu.SMEM)
    vmem = pl.BlockSpec(memory_space=pltpu.VMEM)
    return pl.pallas_call(
        partial(attend_kernel, caps),
        in_specs=[smem, smem, vmem],
        out_specs=vmem,
        out_shape=jax.ShapeDtypeStruct((SERVERS, caps[1], UNIT_PIECE, HEAD_SIZE), jnp.bfloat16),
        scratch_shapes=[
            pltpu.VMEM((1, ROWS), jnp.float32),
            pltpu.VMEM((1, ROWS), jnp.float32),
            pltpu.VMEM((HEAD_SIZE, ROWS), jnp.float32),
            pltpu.VMEM((caps[0], HEAD_SIZE, ROWS), jnp.bfloat16),
        ],
        compiler_params=pltpu.CompilerParams(vmem_limit_bytes=VMEM),
        name="attend",
    )(used, table, units)


def plan(clusters):
    plane = lax.axis_index("z")
    server = lax.axis_index(PLANE)
    clusters = jnp.pad(clusters.T, ((0, SLOT_HEADS - HEADS), (0, 0)))
    tiles = clusters.reshape(SLOT_HEADS, GROUPS, GROUP_TILES)
    index = jnp.arange(GROUP_TILES, dtype=jnp.int32)
    mine, other = tiles[:, :, :, None], tiles[:, :, None, :]
    ahead = (other < mine) | ((other == mine) & (index[None, :] < index[:, None]))
    place = jnp.sum(ahead, axis=3, dtype=jnp.int32)
    at_place = place[:, :, None, :] == index[:, None]
    unit_cluster = jnp.sum(
        jnp.where(at_place[:, :, ::MATCH], tiles[:, :, None, :], 0), axis=3
    ).reshape(SLOT_HEADS, -1)
    units = unit_cluster.shape[1]
    number = jnp.arange(units, dtype=jnp.int32)
    same = unit_cluster[:, :, None] == unit_cluster[:, None, :]
    size = jnp.sum(same, axis=2, dtype=jnp.int32)
    rank = jnp.sum(same & (number[None, :] < number[:, None]), axis=2, dtype=jnp.int32)
    real = jnp.arange(SLOT_HEADS)[:, None] < HEADS
    cut = jnp.where(size >= SPLIT, size * 7 // 10, 0)
    lead = (rank == 0) & real
    whole = jnp.where(lead, size * SCALE + size - cut, 0).reshape(PLANES, UNITS)
    front = jnp.where(lead, cut * SCALE + cut, 0).reshape(PLANES, UNITS)
    tasks = jnp.concatenate([whole, front], axis=1)
    every = jnp.arange(2 * UNITS, dtype=jnp.int32)
    mine, other = tasks[:, :, None], tasks[:, None, :]
    order = jnp.sum(
        (other > mine) | ((other == mine) & (every[None, :] < every[:, None])),
        axis=2,
        dtype=jnp.int32,
    )
    sizes = jnp.sum(
        jnp.where(order[:, None, :] == every[:UNITS, None], tasks[:, None, :], 0), axis=2
    )
    count = jnp.max(jnp.sum(tasks > 0, axis=1, dtype=jnp.int32)).reshape(1)
    sizes = jnp.broadcast_to(
        sizes.T.astype(jnp.float32)[:, :, None], (UNITS, PLANES, 128)
    )
    key, load = assign(count, sizes)
    load = jnp.where(jnp.arange(128)[None, :] < SERVERS, load, 0.0).astype(jnp.int32)
    most = jnp.max(load // SCALE), jnp.max(load % SCALE)
    key = lax.dynamic_slice(key, (0, plane, 0), (UNITS, 1, 1)).reshape(UNITS).astype(jnp.int32)
    load = lax.dynamic_index_in_dim(load, plane, 0, keepdims=False)
    first = plane * PER_PLANE

    def own(array):
        return lax.dynamic_slice_in_dim(array, first, PER_PLANE, 0)

    own_order = lax.dynamic_index_in_dim(order, plane, 0, keepdims=False)
    own_order = own_order.reshape(2, PER_PLANE, 1, units)
    own_rank, own_cut = own(rank), own(cut)
    leader = own(same) & (own_rank == 0)[:, None, :]
    task = jnp.sum(jnp.where(leader, own_order, 0), axis=3).reshape(2, UNITS)
    code = jnp.sum(
        jnp.where(task[:, :, None] == every[:UNITS], key, 0), axis=2
    )
    own_rank, own_cut = own_rank.reshape(UNITS), own_cut.reshape(UNITS)
    owner, before = code % 128, code // 128
    base, query_base = before // SCALE, before % SCALE
    in_front = own_rank < own_cut
    query_owner = jnp.where(in_front, owner[1], owner[0])
    query_slot = jnp.where(in_front, query_base[1] + own_rank, query_base[0] + own_rank - own_cut)
    place = jnp.concatenate(
        [
            query_owner * SCALE + query_slot,
            owner[0] * SCALE + base[0] + own_rank,
            jnp.where(in_front, owner[1] * SCALE + base[1] + own_rank, -1),
        ]
    )
    own_count = jnp.clip(HEADS - first, 0, PER_PLANE) * units
    tile_of = own(
        jnp.sum(jnp.where(at_place, index, 0), axis=3, dtype=jnp.int32)
    ) + jnp.arange(GROUPS, dtype=jnp.int32)[:, None] * GROUP_TILES
    live = every[:UNITS] < own_count
    here = (
        ((query_owner == server) & live)[None, :]
        & (query_slot[None, :] == jnp.arange(LIMIT, dtype=jnp.int32)[:, None])
    )
    table = jnp.where(in_front, base[1], base[0]) * SCALE + own_rank
    table = jnp.sum(jnp.where(here, table[None, :], 0), axis=1)
    mine = jnp.sum(jnp.where(jnp.arange(128) == server, load, 0))
    used = jnp.stack([mine % SCALE, mine // SCALE])
    return (own_count.reshape(1), tile_of.reshape(-1), place, table, used), most


def exchange(caps, arrived, count, tiles, place, table, used):
    packed = pack(caps, count, tiles, place, arrived)
    packed = packed.reshape(SERVERS, -1, UNIT_PIECE, HEAD_SIZE)
    units = lax.all_to_all(packed, PLANE, split_axis=0, concat_axis=0, tiled=True)
    results = attend(caps, used, table, units)
    results = lax.all_to_all(results, PLANE, split_axis=0, concat_axis=0, tiled=True)
    results = results.reshape(SERVERS * caps[1], MATCH, PIECE, HEAD_SIZE)
    return unpack(caps, count, tiles, place, results)


def on_device(queries, keys, values, tile_cluster):
    clusters = jnp.broadcast_to(tile_cluster.reshape(1, 1, HEADS), (SERVERS, 1, HEADS))
    clusters = lax.all_to_all(clusters, PLANE, split_axis=0, concat_axis=0, tiled=True)
    clusters = jnp.broadcast_to(clusters.reshape(1, SERVERS, HEADS), (PLANES, SERVERS, HEADS))
    clusters = lax.all_to_all(clusters, "z", split_axis=0, concat_axis=0, tiled=True)
    clusters = clusters.reshape(PLANES, 2, SERVERS // 2, HEADS)
    clusters = clusters.transpose(1, 0, 2, 3).reshape(TILES, HEADS)
    stacked = jnp.stack([queries, keys, values], axis=1)
    stacked = jnp.pad(stacked, ((0, SLOT_HEADS - HEADS), (0, 0), (0, 0), (0, 0)))
    stacked = stacked.reshape(PLANES, PER_PLANE, 3, 2, SERVERS // 2, PIECE, HEAD_SIZE)
    outgoing = stacked.transpose(3, 0, 4, 1, 2, 5, 6)
    outgoing = outgoing.reshape(TILES, PER_PLANE * 3, PIECE, HEAD_SIZE)
    arrived = lax.all_to_all(outgoing, AXES, split_axis=0, concat_axis=0, tiled=True)
    tables, (most_keys, most_queries) = plan(clusters)
    which = jnp.int32(len(CAPACITIES) - 1)
    for i in range(len(CAPACITIES) - 2, -1, -1):
        fits = (most_keys <= CAPACITIES[i][0]) & (most_queries <= CAPACITIES[i][1])
        which = jnp.where(fits, i, which)
    back = lax.switch(which, [partial(exchange, caps) for caps in CAPACITIES], arrived, *tables)
    back = lax.all_to_all(back, AXES, split_axis=0, concat_axis=0, tiled=True)
    back = back.reshape(2, PLANES, SERVERS // 2, PER_PLANE, PIECE, HEAD_SIZE)
    back = back.transpose(1, 3, 0, 2, 4, 5).reshape(SLOT_HEADS, TILE, HEAD_SIZE)
    return back[:HEADS]


def solution(mesh):
    fine = Mesh(mesh.devices.reshape(SIZES), AXES)
    rows = ("ylo", "z", "yhi", "x", "core")
    return jax.shard_map(
        on_device,
        mesh=fine,
        in_specs=(
            P(None, rows, None),
            P(None, rows, None),
            P(None, rows, None),
            P(None, rows),
        ),
        out_specs=P(None, rows, None),
        check_vma=False,
    )
```

```python
from functools import partial

import jax
import jax.numpy as jnp
from jax import lax
from jax.experimental import pallas as pl
from jax.experimental.pallas import tpu as pltpu
from jax.sharding import Mesh
from jax.sharding import PartitionSpec as P

AXES = ("ylo", "z", "yhi", "x", "core")
PLANE = ("ylo", "yhi", "x", "core")
SIZES = (2, 8, 2, 4, 2)

HEADS = 20
PLANES = 8
PER_PLANE = 3
SLOT_HEADS = PLANES * PER_PLANE
SERVERS = 32
GROUPS = 16
GROUP_TILES = 16
TILES = 256
TILE = 128
MATCH = 4
UNITS = PER_PLANE * GROUPS * GROUP_TILES // MATCH
PIECE = TILE // SERVERS
HEAD_SIZE = 128
LIMIT = 16
CAPACITIES = ((8, 7), (9, 7), (10, 7), (11, 8), (13, 10), (16, 16))
SPLIT = 7
SCALE = 32
STEP = 4
ROWS = MATCH * TILE
UNIT_PIECE = MATCH * PIECE
NEGATIVE = -1e30
VMEM = 56 * 1024 * 1024


def assign_kernel(count_ref, size_ref, key_ref, load_ref):
    lane = lax.broadcasted_iota(jnp.int32, (PLANES, 128), 1)
    lane_number = lane.astype(jnp.float32)
    load_ref[...] = jnp.where(lane < SERVERS, 0.0, 65536.0)

    def step(i, carry):
        load = load_ref[...]
        key = jnp.min(load * 128.0 + lane_number, axis=1, keepdims=True)
        owner = key - jnp.floor(key * (1.0 / 128.0)) * 128.0
        load_ref[...] = load + jnp.where(lane_number == owner, size_ref[i], 0.0)
        key_ref[i] = jnp.broadcast_to(key, (PLANES, 128))
        return carry

    lax.fori_loop(0, count_ref[0], step, 0)


def assign(count, sizes):
    return pl.pallas_call(
        assign_kernel,
        in_specs=[
            pl.BlockSpec(memory_space=pltpu.SMEM),
            pl.BlockSpec(memory_space=pltpu.VMEM),
        ],
        out_specs=[pl.BlockSpec(memory_space=pltpu.VMEM)] * 2,
        out_shape=[
            jax.ShapeDtypeStruct((UNITS, PLANES, 128), jnp.float32),
            jax.ShapeDtypeStruct((PLANES, 128), jnp.float32),
        ],
        compiler_params=pltpu.CompilerParams(vmem_limit_bytes=VMEM),
        name="assign",
    )(count, sizes)


def slab(code, depth, start, width):
    return (code // SCALE) * depth + start + lax.rem(code, SCALE) * width


def pack_kernel(caps, count_ref, tile_ref, place_ref, in_ref, out_ref):
    key_units, query_units = caps
    depth = 2 * key_units + query_units

    def unit(i):
        head = i // (UNITS // PER_PLANE)
        tiles = [tile_ref[i * MATCH + j] for j in range(MATCH)]
        to_query = slab(place_ref[i], depth, 2 * key_units, 1)
        to_keys = slab(place_ref[UNITS + i], depth, 0, 2)
        second = place_ref[2 * UNITS + i]
        for j in range(MATCH):
            out_ref[to_query, j] = in_ref[tiles[j], head * 3]
            out_ref[to_keys, j] = in_ref[tiles[j], head * 3 + 1]
            out_ref[to_keys + 1, j] = in_ref[tiles[j], head * 3 + 2]

        @pl.when(second >= 0)
        def _():
            also = slab(second, depth, 0, 2)
            for j in range(MATCH):
                out_ref[also, j] = in_ref[tiles[j], head * 3 + 1]
                out_ref[also + 1, j] = in_ref[tiles[j], head * 3 + 2]

    def some(i, carry):
        for k in range(STEP):
            unit(i * STEP + k)
        return carry

    lax.fori_loop(0, count_ref[0] // STEP, some, 0)


def pack(caps, count, tiles, place, arrived):
    smem = pl.BlockSpec(memory_space=pltpu.SMEM)
    vmem = pl.BlockSpec(memory_space=pltpu.VMEM)
    return pl.pallas_call(
        partial(pack_kernel, caps),
        in_specs=[smem, smem, smem, vmem],
        out_specs=vmem,
        out_shape=jax.ShapeDtypeStruct(
            (SERVERS * (2 * caps[0] + caps[1]), MATCH, PIECE, HEAD_SIZE), jnp.bfloat16
        ),
        compiler_params=pltpu.CompilerParams(vmem_limit_bytes=VMEM),
        name="pack_units",
    )(count, tiles, place, arrived)


def unpack_kernel(caps, count_ref, tile_ref, place_ref, in_ref, out_ref):
    def some(i, carry):
        for k in range(STEP):
            unit = i * STEP + k
            slot = slab(place_ref[unit], caps[1], 0, 1)
            head = unit // (UNITS // PER_PLANE)
            for j in range(MATCH):
                out_ref[tile_ref[unit * MATCH + j], head] = in_ref[slot, j]
        return carry

    lax.fori_loop(0, count_ref[0] // STEP, some, 0)


def unpack(caps, count, tiles, place, results):
    smem = pl.BlockSpec(memory_space=pltpu.SMEM)
    vmem = pl.BlockSpec(memory_space=pltpu.VMEM)
    return pl.pallas_call(
        partial(unpack_kernel, caps),
        in_specs=[smem, smem, smem, vmem],
        out_specs=vmem,
        out_shape=jax.ShapeDtypeStruct((TILES, PER_PLANE, PIECE, HEAD_SIZE), jnp.bfloat16),
        compiler_params=pltpu.CompilerParams(vmem_limit_bytes=VMEM),
        name="unpack_units",
    )(count, tiles, place, results)


def row_key(shape, dim):
    row = lax.broadcasted_iota(jnp.int32, shape, dim)
    piece = row // UNIT_PIECE
    tile = lax.rem(row // PIECE, MATCH)
    return tile * TILE + piece * PIECE + lax.rem(row, PIECE)


def attend_kernel(caps, used_ref, table_ref, in_ref, out_ref, peak_ref, total_ref, sum_ref, turned_ref):
    factor = HEAD_SIZE**-0.5

    def rows(which):
        return in_ref[:, which].reshape(ROWS, HEAD_SIZE)

    def turn(unit, carry):
        turned_ref[unit] = rows(2 * unit + 1).T
        return carry

    lax.fori_loop(0, used_ref[1], turn, 0)

    def one_query_unit(slot, carry):
        code = table_ref[slot]
        first = code // SCALE
        last = first + lax.rem(code, SCALE)
        query = rows(2 * caps[0] + slot)

        def scores_of(unit):
            return lax.dot_general(
                rows(2 * unit), query, (((1,), (1,)), ((), ())), preferred_element_type=jnp.float32
            )

        def weigh(unit, weights):
            return jnp.dot(
                turned_ref[unit], weights.astype(jnp.bfloat16), preferred_element_type=jnp.float32
            )

        def exponential(scores, peak):
            return jnp.exp((scores - peak) * factor)

        def fold(units):
            peak, total, mixed = peak_ref[...], total_ref[...], sum_ref[...]
            for unit, scores in [(unit, scores_of(unit)) for unit in units]:
                old, peak = peak, jnp.maximum(peak, jnp.max(scores, axis=0, keepdims=True))
                weights = exponential(scores, peak)
                keep = exponential(old, peak)
                total = total * keep + jnp.sum(weights, axis=0, keepdims=True)
                mixed = mixed * keep + weigh(unit, weights)
            peak_ref[...], total_ref[...], sum_ref[...] = peak, total, mixed

        visible = row_key((ROWS, 1), 0) <= row_key((1, ROWS), 1)
        scores = jnp.where(visible, scores_of(last), NEGATIVE)
        peak = jnp.max(scores, axis=0, keepdims=True)
        weights = exponential(scores, peak)
        peak_ref[...] = peak
        total_ref[...] = jnp.sum(weights, axis=0, keepdims=True)
        sum_ref[...] = weigh(last, weights)
        odd = lax.rem(last - first, 2)

        @pl.when(odd == 1)
        def _():
            fold([first])

        def two(i, carry):
            fold([first + odd + 2 * i, first + odd + 2 * i + 1])
            return carry

        lax.fori_loop(0, (last - first) // 2, two, 0)
        result = (sum_ref[...] / total_ref[...]).T.astype(jnp.bfloat16)
        out_ref[:, slot] = result.reshape(SERVERS, UNIT_PIECE, HEAD_SIZE)
        return carry

    lax.fori_loop(0, used_ref[0], one_query_unit, 0)


def attend(caps, used, table, units):
    smem = pl.BlockSpec(memory_space=pltpu.SMEM)
    vmem = pl.BlockSpec(memory_space=pltpu.VMEM)
    return pl.pallas_call(
        partial(attend_kernel, caps),
        in_specs=[smem, smem, vmem],
        out_specs=vmem,
        out_shape=jax.ShapeDtypeStruct((SERVERS, caps[1], UNIT_PIECE, HEAD_SIZE), jnp.bfloat16),
        scratch_shapes=[
            pltpu.VMEM((1, ROWS), jnp.float32),
            pltpu.VMEM((1, ROWS), jnp.float32),
            pltpu.VMEM((HEAD_SIZE, ROWS), jnp.float32),
            pltpu.VMEM((caps[0], HEAD_SIZE, ROWS), jnp.bfloat16),
        ],
        compiler_params=pltpu.CompilerParams(vmem_limit_bytes=VMEM),
        name="attend",
    )(used, table, units)


def plan(clusters):
    plane = lax.axis_index("z")
    server = lax.axis_index(PLANE)
    clusters = jnp.pad(clusters.T, ((0, SLOT_HEADS - HEADS), (0, 0)))
    tiles = clusters.reshape(SLOT_HEADS, GROUPS, GROUP_TILES)
    index = jnp.arange(GROUP_TILES, dtype=jnp.int32)
    mine, other = tiles[:, :, :, None], tiles[:, :, None, :]
    ahead = (other < mine) | ((other == mine) & (index[None, :] < index[:, None]))
    place = jnp.sum(ahead, axis=3, dtype=jnp.int32)
    at_place = place[:, :, None, :] == index[:, None]
    unit_cluster = jnp.sum(
        jnp.where(at_place[:, :, ::MATCH], tiles[:, :, None, :], 0), axis=3
    ).reshape(SLOT_HEADS, -1)
    units = unit_cluster.shape[1]
    number = jnp.arange(units, dtype=jnp.int32)
    same = unit_cluster[:, :, None] == unit_cluster[:, None, :]
    size = jnp.sum(same, axis=2, dtype=jnp.int32)
    rank = jnp.sum(same & (number[None, :] < number[:, None]), axis=2, dtype=jnp.int32)
    real = jnp.arange(SLOT_HEADS)[:, None] < HEADS
    cut = jnp.where(size >= SPLIT, size * 7 // 10, 0)
    lead = (rank == 0) & real
    whole = jnp.where(lead, size * SCALE + size - cut, 0).reshape(PLANES, UNITS)
    front = jnp.where(lead, cut * SCALE + cut, 0).reshape(PLANES, UNITS)
    tasks = jnp.concatenate([whole, front], axis=1)
    every = jnp.arange(2 * UNITS, dtype=jnp.int32)
    mine, other = tasks[:, :, None], tasks[:, None, :]
    order = jnp.sum(
        (other > mine) | ((other == mine) & (every[None, :] < every[:, None])),
        axis=2,
        dtype=jnp.int32,
    )
    sizes = jnp.sum(
        jnp.where(order[:, None, :] == every[:UNITS, None], tasks[:, None, :], 0), axis=2
    )
    count = jnp.max(jnp.sum(tasks > 0, axis=1, dtype=jnp.int32)).reshape(1)
    sizes = jnp.broadcast_to(
        sizes.T.astype(jnp.float32)[:, :, None], (UNITS, PLANES, 128)
    )
    key, load = assign(count, sizes)
    load = jnp.where(jnp.arange(128)[None, :] < SERVERS, load, 0.0).astype(jnp.int32)
    most = jnp.max(load // SCALE), jnp.max(load % SCALE)
    key = lax.dynamic_slice(key, (0, plane, 0), (UNITS, 1, 1)).reshape(UNITS).astype(jnp.int32)
    load = lax.dynamic_index_in_dim(load, plane, 0, keepdims=False)
    first = plane * PER_PLANE

    def own(array):
        return lax.dynamic_slice_in_dim(array, first, PER_PLANE, 0)

    own_order = lax.dynamic_index_in_dim(order, plane, 0, keepdims=False)
    own_order = own_order.reshape(2, PER_PLANE, 1, units)
    own_rank, own_cut = own(rank), own(cut)
    leader = own(same) & (own_rank == 0)[:, None, :]
    task = jnp.sum(jnp.where(leader, own_order, 0), axis=3).reshape(2, UNITS)
    code = jnp.sum(
        jnp.where(task[:, :, None] == every[:UNITS], key, 0), axis=2
    )
    own_rank, own_cut = own_rank.reshape(UNITS), own_cut.reshape(UNITS)
    owner, before = code % 128, code // 128
    base, query_base = before // SCALE, before % SCALE
    in_front = own_rank < own_cut
    query_owner = jnp.where(in_front, owner[1], owner[0])
    query_slot = jnp.where(in_front, query_base[1] + own_rank, query_base[0] + own_rank - own_cut)
    place = jnp.concatenate(
        [
            query_owner * SCALE + query_slot,
            owner[0] * SCALE + base[0] + own_rank,
            jnp.where(in_front, owner[1] * SCALE + base[1] + own_rank, -1),
        ]
    )
    own_count = jnp.clip(HEADS - first, 0, PER_PLANE) * units
    tile_of = own(
        jnp.sum(jnp.where(at_place, index, 0), axis=3, dtype=jnp.int32)
    ) + jnp.arange(GROUPS, dtype=jnp.int32)[:, None] * GROUP_TILES
    live = every[:UNITS] < own_count
    here = (
        ((query_owner == server) & live)[None, :]
        & (query_slot[None, :] == jnp.arange(LIMIT, dtype=jnp.int32)[:, None])
    )
    table = jnp.where(in_front, base[1], base[0]) * SCALE + own_rank
    table = jnp.sum(jnp.where(here, table[None, :], 0), axis=1)
    mine = jnp.sum(jnp.where(jnp.arange(128) == server, load, 0))
    used = jnp.stack([mine % SCALE, mine // SCALE])
    return (own_count.reshape(1), tile_of.reshape(-1), place, table, used), most


def exchange(caps, arrived, count, tiles, place, table, used):
    packed = pack(caps, count, tiles, place, arrived)
    packed = packed.reshape(SERVERS, -1, UNIT_PIECE, HEAD_SIZE)
    units = lax.all_to_all(packed, PLANE, split_axis=0, concat_axis=0, tiled=True)
    results = attend(caps, used, table, units)
    results = lax.all_to_all(results, PLANE, split_axis=0, concat_axis=0, tiled=True)
    results = results.reshape(SERVERS * caps[1], MATCH, PIECE, HEAD_SIZE)
    return unpack(caps, count, tiles, place, results)


def gather_by_permutes(blocks, axes):
    size = lax.axis_size(axes)
    me = lax.axis_index(axes)
    parts = [blocks] + [
        lax.ppermute(blocks, axes, [(i, (i - shift) % size) for i in range(size)])
        for shift in range(1, size)
    ]
    index = jnp.arange(size, dtype=jnp.int32)
    chosen = ((index[:, None] - me + size) % size == index).astype(jnp.int32)
    chosen = lax.optimization_barrier(chosen)
    ordered = sum(
        chosen[:, j].reshape((size,) + (1,) * blocks.ndim) * part for j, part in enumerate(parts)
    )
    return lax.optimization_barrier(ordered.reshape((-1,) + blocks.shape[1:]))


def on_device(queries, keys, values, tile_cluster):
    clusters = gather_by_permutes(tile_cluster.reshape(1, 1, HEADS), "z")
    clusters = gather_by_permutes(clusters.reshape(1, PLANES, HEADS), ("ylo", "yhi"))
    clusters = clusters.reshape(1, 4 * PLANES, HEADS)
    stacked = jnp.stack([queries, keys, values], axis=1)
    stacked = jnp.pad(stacked, ((0, SLOT_HEADS - HEADS), (0, 0), (0, 0), (0, 0)))
    stacked = stacked.reshape(PLANES, PER_PLANE, 3, 2, SERVERS // 2, PIECE, HEAD_SIZE)
    outgoing = stacked.transpose(3, 0, 4, 1, 2, 5, 6)
    outgoing = outgoing.reshape(TILES, PER_PLANE * 3, PIECE, HEAD_SIZE)
    clusters, outgoing = lax.optimization_barrier((clusters, outgoing))
    arrived = lax.all_to_all(outgoing, AXES, split_axis=0, concat_axis=0, tiled=True)
    clusters = gather_by_permutes(clusters, ("x", "core"))
    clusters = clusters.reshape(8, 2, 2, PLANES, HEADS)
    clusters = clusters.transpose(1, 3, 2, 0, 4).reshape(TILES, HEADS)
    tables, (most_keys, most_queries) = plan(clusters)
    which = jnp.int32(len(CAPACITIES) - 1)
    for i in range(len(CAPACITIES) - 2, -1, -1):
        fits = (most_keys <= CAPACITIES[i][0]) & (most_queries <= CAPACITIES[i][1])
        which = jnp.where(fits, i, which)
    back = lax.switch(which, [partial(exchange, caps) for caps in CAPACITIES], arrived, *tables)
    back = lax.all_to_all(back, AXES, split_axis=0, concat_axis=0, tiled=True)
    back = back.reshape(2, PLANES, SERVERS // 2, PER_PLANE, PIECE, HEAD_SIZE)
    back = back.transpose(1, 3, 0, 2, 4, 5).reshape(SLOT_HEADS, TILE, HEAD_SIZE)
    return back[:HEADS]


def solution(mesh):
    fine = Mesh(mesh.devices.reshape(SIZES), AXES)
    rows = ("ylo", "z", "yhi", "x", "core")
    return jax.shard_map(
        on_device,
        mesh=fine,
        in_specs=(
            P(None, rows, None),
            P(None, rows, None),
            P(None, rows, None),
            P(None, rows),
        ),
        out_specs=P(None, rows, None),
        check_vma=False,
    )
```

```python
from functools import partial

import jax
import jax.numpy as jnp
from jax import lax
from jax.experimental import pallas as pl
from jax.experimental.pallas import tpu as pltpu
from jax.sharding import Mesh
from jax.sharding import PartitionSpec as P

AXES = ("ylo", "z", "yhi", "x", "core")
PLANE = ("ylo", "yhi", "x", "core")
SIZES = (2, 8, 2, 4, 2)

HEADS = 20
PLANES = 8
PER_PLANE = 3
SLOT_HEADS = PLANES * PER_PLANE
SERVERS = 32
GROUPS = 16
GROUP_TILES = 16
TILES = 256
TILE = 128
MATCH = 4
UNITS = PER_PLANE * GROUPS * GROUP_TILES // MATCH
PIECE = TILE // SERVERS
HEAD_SIZE = 128
LIMIT = 16
CAPACITIES = ((8, 7), (9, 7), (10, 7), (11, 8), (13, 10), (16, 16))
SPLIT = 7
SCALE = 32
STEP = 4
ROWS = MATCH * TILE
UNIT_PIECE = MATCH * PIECE
NEGATIVE = -1e30
VMEM = 56 * 1024 * 1024


def assign_kernel(count_ref, size_ref, key_ref, load_ref):
    lane = lax.broadcasted_iota(jnp.int32, (PLANES, 128), 1)
    lane_number = lane.astype(jnp.float32)
    load_ref[...] = jnp.where(lane < SERVERS, 0.0, 65536.0)

    def step(i, carry):
        load = load_ref[...]
        key = jnp.min(load * 128.0 + lane_number, axis=1, keepdims=True)
        owner = key - jnp.floor(key * (1.0 / 128.0)) * 128.0
        load_ref[...] = load + jnp.where(lane_number == owner, size_ref[i], 0.0)
        key_ref[i] = jnp.broadcast_to(key, (PLANES, 128))
        return carry

    lax.fori_loop(0, count_ref[0], step, 0)


def assign(count, sizes):
    return pl.pallas_call(
        assign_kernel,
        in_specs=[
            pl.BlockSpec(memory_space=pltpu.SMEM),
            pl.BlockSpec(memory_space=pltpu.VMEM),
        ],
        out_specs=[pl.BlockSpec(memory_space=pltpu.VMEM)] * 2,
        out_shape=[
            jax.ShapeDtypeStruct((UNITS, PLANES, 128), jnp.float32),
            jax.ShapeDtypeStruct((PLANES, 128), jnp.float32),
        ],
        compiler_params=pltpu.CompilerParams(vmem_limit_bytes=VMEM),
        name="assign",
    )(count, sizes)


def slab(code, depth, start, width):
    owner = lax.shift_right_logical(code, SCALE.bit_length() - 1)
    return owner * depth + start + (code & (SCALE - 1)) * width


def move_units(steps, tile_ref, move):
    def some(i, carry):
        moves = []
        for k in range(STEP):
            unit = i * STEP + k
            head = lax.shift_right_logical(unit, (UNITS // PER_PLANE).bit_length() - 1)
            moves += move(unit, head, [tile_ref[unit * MATCH + j] for j in range(MATCH)])
        pieces = [load() for load, _ in moves]
        for piece, (_, store) in zip(pieces, moves):
            store(piece)
        return carry

    lax.fori_loop(0, steps, some, 0)


def mover(in_ref, source, out_ref, target):
    def store(piece):
        out_ref[target] = piece

    return lambda: in_ref[source], store


def pack_kernel(caps, count_ref, tile_ref, place_ref, in_ref, out_ref):
    key_units, query_units = caps
    depth = 2 * key_units + query_units

    def first(unit, head, tiles):
        to_query = slab(place_ref[unit], depth, 2 * key_units, 1)
        to_keys = slab(place_ref[UNITS + unit], depth, 0, 2)
        return [
            mover(in_ref, (tile, head * 3 + s), out_ref, (slot, j))
            for j, tile in enumerate(tiles)
            for s, slot in enumerate((to_query, to_keys, to_keys + 1))
        ]

    move_units(lax.shift_right_logical(count_ref[0], STEP.bit_length() - 1), tile_ref, first)

    def again(unit, carry):
        second = place_ref[2 * UNITS + unit]

        @pl.when(second >= 0)
        def _():
            head = lax.shift_right_logical(unit, (UNITS // PER_PLANE).bit_length() - 1)
            also = slab(second, depth, 0, 2)
            tiles = [tile_ref[unit * MATCH + j] for j in range(MATCH)]
            pieces = [in_ref[tile, head * 3 + s] for tile in tiles for s in (1, 2)]
            for i, piece in enumerate(pieces):
                out_ref[also + i % 2, i // 2] = piece

        return carry

    lax.fori_loop(0, count_ref[0], again, 0)


def pack(caps, count, tiles, place, arrived):
    smem = pl.BlockSpec(memory_space=pltpu.SMEM)
    vmem = pl.BlockSpec(memory_space=pltpu.VMEM)
    return pl.pallas_call(
        partial(pack_kernel, caps),
        in_specs=[smem, smem, smem, vmem],
        out_specs=vmem,
        out_shape=jax.ShapeDtypeStruct(
            (SERVERS * (2 * caps[0] + caps[1]), MATCH, PIECE, HEAD_SIZE), jnp.bfloat16
        ),
        compiler_params=pltpu.CompilerParams(vmem_limit_bytes=VMEM),
        name="pack_units",
    )(count, tiles, place, arrived)


def unpack_kernel(caps, count_ref, tile_ref, place_ref, in_ref, out_ref):
    def back(unit, head, tiles):
        slot = slab(place_ref[unit], caps[1], 0, 1)
        return [mover(in_ref, (slot, j), out_ref, (tile, head)) for j, tile in enumerate(tiles)]

    move_units(lax.shift_right_logical(count_ref[0], STEP.bit_length() - 1), tile_ref, back)


def unpack(caps, count, tiles, place, results):
    smem = pl.BlockSpec(memory_space=pltpu.SMEM)
    vmem = pl.BlockSpec(memory_space=pltpu.VMEM)
    return pl.pallas_call(
        partial(unpack_kernel, caps),
        in_specs=[smem, smem, smem, vmem],
        out_specs=vmem,
        out_shape=jax.ShapeDtypeStruct((TILES, PER_PLANE, PIECE, HEAD_SIZE), jnp.bfloat16),
        compiler_params=pltpu.CompilerParams(vmem_limit_bytes=VMEM),
        name="unpack_units",
    )(count, tiles, place, results)


def row_key(shape, dim):
    row = lax.broadcasted_iota(jnp.int32, shape, dim)
    piece = row // UNIT_PIECE
    tile = lax.rem(row // PIECE, MATCH)
    return tile * TILE + piece * PIECE + lax.rem(row, PIECE)


def attend_kernel(
    caps, used_ref, table_ref, in_ref, out_ref, peak_ref, total_ref, sum_ref, turned_ref, *score_refs
):
    factor = HEAD_SIZE**-0.5 * 1.4426950408889634

    def rows(which):
        return in_ref[:, which].reshape(ROWS, HEAD_SIZE)

    def turn(unit, carry):
        turned_ref[unit] = rows(2 * unit + 1).T
        return carry

    lax.fori_loop(0, used_ref[1], turn, 0)

    def one_query_unit(slot, carry):
        code = table_ref[slot]
        first = lax.shift_right_logical(code, SCALE.bit_length() - 1)
        earlier = code & (SCALE - 1)
        last = first + earlier
        query = rows(2 * caps[0] + slot)

        def scores_of(unit):
            return lax.dot_general(
                rows(2 * unit), query, (((1,), (1,)), ((), ())), preferred_element_type=jnp.float32
            )

        def unit_at(step):
            return jnp.where(step == 0, last, jnp.minimum(first + step - 1, last))

        def fold(step, now):
            score_refs[1 - now][...] = scores_of(unit_at(step + 1))
            scores = score_refs[now][...]
            old = peak_ref[...]
            peak = jnp.maximum(old, jnp.max(scores, axis=0, keepdims=True))
            weights = jnp.exp2((scores - peak) * factor)
            keep = jnp.exp2((old - peak) * factor)
            peak_ref[...] = peak
            total_ref[...] = total_ref[...] * keep + jnp.sum(weights, axis=0, keepdims=True)
            sum_ref[...] = sum_ref[...] * keep + jnp.dot(
                turned_ref[unit_at(step)],
                weights.astype(jnp.bfloat16),
                preferred_element_type=jnp.float32,
            )

        visible = row_key((ROWS, 1), 0) <= row_key((1, ROWS), 1)
        score_refs[0][...] = jnp.where(visible, scores_of(last), NEGATIVE)
        peak_ref[...] = jnp.full(peak_ref.shape, NEGATIVE, jnp.float32)
        total_ref[...] = jnp.zeros(total_ref.shape, jnp.float32)
        sum_ref[...] = jnp.zeros(sum_ref.shape, jnp.float32)

        def two(i, carry):
            fold(2 * i, 0)
            fold(2 * i + 1, 1)
            return carry

        lax.fori_loop(0, lax.shift_right_logical(earlier + 1, 1), two, 0)

        @pl.when((earlier & 1) == 0)
        def _():
            fold(earlier, 0)

        result = (sum_ref[...] / total_ref[...]).T.astype(jnp.bfloat16)
        out_ref[:, slot] = result.reshape(SERVERS, UNIT_PIECE, HEAD_SIZE)
        return carry

    lax.fori_loop(0, used_ref[0], one_query_unit, 0)


def attend(caps, used, table, units):
    smem = pl.BlockSpec(memory_space=pltpu.SMEM)
    vmem = pl.BlockSpec(memory_space=pltpu.VMEM)
    return pl.pallas_call(
        partial(attend_kernel, caps),
        in_specs=[smem, smem, vmem],
        out_specs=vmem,
        out_shape=jax.ShapeDtypeStruct((SERVERS, caps[1], UNIT_PIECE, HEAD_SIZE), jnp.bfloat16),
        scratch_shapes=[
            pltpu.VMEM((1, ROWS), jnp.float32),
            pltpu.VMEM((1, ROWS), jnp.float32),
            pltpu.VMEM((HEAD_SIZE, ROWS), jnp.float32),
            pltpu.VMEM((caps[0], HEAD_SIZE, ROWS), jnp.bfloat16),
            pltpu.VMEM((ROWS, ROWS), jnp.float32),
            pltpu.VMEM((ROWS, ROWS), jnp.float32),
        ],
        compiler_params=pltpu.CompilerParams(vmem_limit_bytes=VMEM),
        name="attend",
    )(used, table, units)


def plan(clusters):
    plane = lax.axis_index("z")
    server = lax.axis_index(PLANE)
    clusters = jnp.pad(clusters.T, ((0, SLOT_HEADS - HEADS), (0, 0)))
    tiles = clusters.reshape(SLOT_HEADS, GROUPS, GROUP_TILES)
    index = jnp.arange(GROUP_TILES, dtype=jnp.int32)
    mine, other = tiles[:, :, :, None], tiles[:, :, None, :]
    ahead = (other < mine) | ((other == mine) & (index[None, :] < index[:, None]))
    place = jnp.sum(ahead, axis=3, dtype=jnp.int32)
    at_place = place[:, :, None, :] == index[:, None]
    unit_cluster = jnp.sum(
        jnp.where(at_place[:, :, ::MATCH], tiles[:, :, None, :], 0), axis=3
    ).reshape(SLOT_HEADS, -1)
    units = unit_cluster.shape[1]
    number = jnp.arange(units, dtype=jnp.int32)
    same = unit_cluster[:, :, None] == unit_cluster[:, None, :]
    size = jnp.sum(same, axis=2, dtype=jnp.int32)
    rank = jnp.sum(same & (number[None, :] < number[:, None]), axis=2, dtype=jnp.int32)
    real = jnp.arange(SLOT_HEADS)[:, None] < HEADS
    cut = jnp.where(size >= SPLIT, size * 7 // 10, 0)
    lead = (rank == 0) & real
    whole = jnp.where(lead, size * SCALE + size - cut, 0).reshape(PLANES, UNITS)
    front = jnp.where(lead, cut * SCALE + cut, 0).reshape(PLANES, UNITS)
    tasks = jnp.concatenate([whole, front], axis=1)
    every = jnp.arange(2 * UNITS, dtype=jnp.int32)
    mine, other = tasks[:, :, None], tasks[:, None, :]
    order = jnp.sum(
        (other > mine) | ((other == mine) & (every[None, :] < every[:, None])),
        axis=2,
        dtype=jnp.int32,
    )
    sizes = jnp.sum(
        jnp.where(order[:, None, :] == every[:UNITS, None], tasks[:, None, :], 0), axis=2
    )
    count = jnp.max(jnp.sum(tasks > 0, axis=1, dtype=jnp.int32)).reshape(1)
    sizes = jnp.broadcast_to(
        sizes.T.astype(jnp.float32)[:, :, None], (UNITS, PLANES, 128)
    )
    key, load = assign(count, sizes)
    load = jnp.where(jnp.arange(128)[None, :] < SERVERS, load, 0.0).astype(jnp.int32)
    most = jnp.max(load // SCALE), jnp.max(load % SCALE)
    key = lax.dynamic_slice(key, (0, plane, 0), (UNITS, 1, 1)).reshape(UNITS).astype(jnp.int32)
    load = lax.dynamic_index_in_dim(load, plane, 0, keepdims=False)
    first = plane * PER_PLANE

    def own(array):
        return lax.dynamic_slice_in_dim(array, first, PER_PLANE, 0)

    own_order = lax.dynamic_index_in_dim(order, plane, 0, keepdims=False)
    own_order = own_order.reshape(2, PER_PLANE, 1, units)
    own_rank, own_cut = own(rank), own(cut)
    leader = own(same) & (own_rank == 0)[:, None, :]
    task = jnp.sum(jnp.where(leader, own_order, 0), axis=3).reshape(2, UNITS)
    code = jnp.sum(
        jnp.where(task[:, :, None] == every[:UNITS], key, 0), axis=2
    )
    own_rank, own_cut = own_rank.reshape(UNITS), own_cut.reshape(UNITS)
    owner, before = code % 128, code // 128
    base, query_base = before // SCALE, before % SCALE
    in_front = own_rank < own_cut
    query_owner = jnp.where(in_front, owner[1], owner[0])
    query_slot = jnp.where(in_front, query_base[1] + own_rank, query_base[0] + own_rank - own_cut)
    place = jnp.concatenate(
        [
            query_owner * SCALE + query_slot,
            owner[0] * SCALE + base[0] + own_rank,
            jnp.where(in_front, owner[1] * SCALE + base[1] + own_rank, -1),
        ]
    )
    own_count = jnp.clip(HEADS - first, 0, PER_PLANE) * units
    tile_of = own(
        jnp.sum(jnp.where(at_place, index, 0), axis=3, dtype=jnp.int32)
    ) + jnp.arange(GROUPS, dtype=jnp.int32)[:, None] * GROUP_TILES
    live = every[:UNITS] < own_count
    here = (
        ((query_owner == server) & live)[None, :]
        & (query_slot[None, :] == jnp.arange(LIMIT, dtype=jnp.int32)[:, None])
    )
    table = jnp.where(in_front, base[1], base[0]) * SCALE + own_rank
    table = jnp.sum(jnp.where(here, table[None, :], 0), axis=1)
    mine = jnp.sum(jnp.where(jnp.arange(128) == server, load, 0))
    used = jnp.stack([mine % SCALE, mine // SCALE])
    return (own_count.reshape(1), tile_of.reshape(-1), place, table, used), most


def exchange(caps, arrived, count, tiles, place, table, used):
    packed = pack(caps, count, tiles, place, arrived)
    packed = packed.reshape(SERVERS, -1, UNIT_PIECE, HEAD_SIZE)
    units = lax.all_to_all(packed, PLANE, split_axis=0, concat_axis=0, tiled=True)
    results = attend(caps, used, table, units)
    results = lax.all_to_all(results, PLANE, split_axis=0, concat_axis=0, tiled=True)
    results = results.reshape(SERVERS * caps[1], MATCH, PIECE, HEAD_SIZE)
    return unpack(caps, count, tiles, place, results)


def on_device(queries, keys, values, tile_cluster):
    clusters = jnp.broadcast_to(tile_cluster.reshape(1, 1, HEADS), (TILES, 1, HEADS))
    clusters = lax.all_to_all(clusters, AXES, split_axis=0, concat_axis=0, tiled=True)
    clusters = clusters.reshape(TILES, HEADS)
    stacked = jnp.stack([queries, keys, values], axis=1)
    stacked = jnp.pad(stacked, ((0, SLOT_HEADS - HEADS), (0, 0), (0, 0), (0, 0)))
    stacked = stacked.reshape(PLANES, PER_PLANE, 3, 2, SERVERS // 2, PIECE, HEAD_SIZE)
    outgoing = stacked.transpose(3, 0, 4, 1, 2, 5, 6)
    outgoing = outgoing.reshape(TILES, PER_PLANE * 3, PIECE, HEAD_SIZE)
    arrived = lax.all_to_all(outgoing, AXES, split_axis=0, concat_axis=0, tiled=True)
    tables, (most_keys, most_queries) = plan(clusters)
    which = jnp.int32(len(CAPACITIES) - 1)
    for i in range(len(CAPACITIES) - 2, -1, -1):
        fits = (most_keys <= CAPACITIES[i][0]) & (most_queries <= CAPACITIES[i][1])
        which = jnp.where(fits, i, which)
    back = lax.switch(which, [partial(exchange, caps) for caps in CAPACITIES], arrived, *tables)
    back = lax.all_to_all(back, AXES, split_axis=0, concat_axis=0, tiled=True)
    back = back.reshape(2, PLANES, SERVERS // 2, PER_PLANE, PIECE, HEAD_SIZE)
    back = back.transpose(1, 3, 0, 2, 4, 5).reshape(SLOT_HEADS, TILE, HEAD_SIZE)
    return back[:HEADS]


def solution(mesh):
    fine = Mesh(mesh.devices.reshape(SIZES), AXES)
    rows = ("ylo", "z", "yhi", "x", "core")
    return jax.shard_map(
        on_device,
        mesh=fine,
        in_specs=(
            P(None, rows, None),
            P(None, rows, None),
            P(None, rows, None),
            P(None, rows),
        ),
        out_specs=P(None, rows, None),
        check_vma=False,
    )
```

```python
from functools import partial

import jax
import jax.numpy as jnp
from jax import lax
from jax.experimental import pallas as pl
from jax.experimental.pallas import tpu as pltpu
from jax.sharding import Mesh
from jax.sharding import PartitionSpec as P

AXES = ("ylo", "z", "yhi", "x", "core")
PLANE = ("ylo", "yhi", "x", "core")
SIZES = (2, 8, 2, 4, 2)

HEADS = 20
PLANES = 8
PER_PLANE = 3
SLOT_HEADS = PLANES * PER_PLANE
SERVERS = 32
GROUPS = 16
GROUP_TILES = 16
TILES = 256
TILE = 128
MATCH = 4
UNITS = PER_PLANE * GROUPS * GROUP_TILES // MATCH
PIECE = TILE // SERVERS
HEAD_SIZE = 128
CAPACITIES = ((21, 7), (23, 7), (26, 8), (32, 11), (64, 22))
SPLIT = 7
SCALE = 32
STEP = 4
ROWS = MATCH * TILE
UNIT_PIECE = MATCH * PIECE
NEGATIVE = -1e30
VMEM = 56 * 1024 * 1024


def assign_kernel(count_ref, size_ref, key_ref, load_ref):
    lane = lax.broadcasted_iota(jnp.int32, (PLANES, 128), 1)
    lane_number = lane.astype(jnp.float32)
    load_ref[...] = jnp.where(lane < SERVERS, 0.0, 65536.0)

    def step(i, carry):
        load = load_ref[...]
        key = jnp.min(load * 128.0 + lane_number, axis=1, keepdims=True)
        owner = key - jnp.floor(key * (1.0 / 128.0)) * 128.0
        load_ref[...] = load + jnp.where(lane_number == owner, size_ref[i], 0.0)
        key_ref[i] = jnp.broadcast_to(key, (PLANES, 128))
        return carry

    lax.fori_loop(0, count_ref[0], step, 0)


def assign(count, sizes):
    return pl.pallas_call(
        assign_kernel,
        in_specs=[
            pl.BlockSpec(memory_space=pltpu.SMEM),
            pl.BlockSpec(memory_space=pltpu.VMEM),
        ],
        out_specs=[pl.BlockSpec(memory_space=pltpu.VMEM)] * 2,
        out_shape=[
            jax.ShapeDtypeStruct((UNITS, PLANES, 128), jnp.float32),
            jax.ShapeDtypeStruct((PLANES, 128), jnp.float32),
        ],
        compiler_params=pltpu.CompilerParams(vmem_limit_bytes=VMEM),
        name="assign",
    )(count, sizes)


def slab(code, depth, start, width):
    owner = lax.shift_right_logical(code, SCALE.bit_length() - 1)
    return owner * depth + start + (code & (SCALE - 1)) * width


def move_units(steps, tile_ref, move):
    def some(i, carry):
        moves = []
        for k in range(STEP):
            unit = i * STEP + k
            head = lax.shift_right_logical(unit, (UNITS // PER_PLANE).bit_length() - 1)
            moves += move(unit, head, [tile_ref[unit * MATCH + j] for j in range(MATCH)])
        pieces = [load() for load, _ in moves]
        for piece, (_, store) in zip(pieces, moves):
            store(piece)
        return carry

    lax.fori_loop(0, steps, some, 0)


def mover(in_ref, source, out_ref, target):
    def store(piece):
        out_ref[target] = piece

    return lambda: in_ref[source], store


def pack_kernel(caps, count_ref, tile_ref, place_ref, in_ref, out_ref):
    depth = caps[0]

    def first(unit, head, tiles):
        to_query = slab(place_ref[unit], depth, depth - 1, -1)
        to_keys = slab(place_ref[UNITS + unit], depth, 0, 2)
        return [
            mover(in_ref, (tile, head * 3 + s), out_ref, (slot, j))
            for j, tile in enumerate(tiles)
            for s, slot in enumerate((to_query, to_keys, to_keys + 1))
        ]

    move_units(lax.shift_right_logical(count_ref[0], STEP.bit_length() - 1), tile_ref, first)

    def again(i, carry):
        unit = place_ref[3 * UNITS + i]
        head = lax.shift_right_logical(unit, (UNITS // PER_PLANE).bit_length() - 1)
        also = slab(place_ref[2 * UNITS + unit], depth, 0, 2)
        tiles = [tile_ref[unit * MATCH + j] for j in range(MATCH)]
        pieces = [in_ref[tile, head * 3 + s] for tile in tiles for s in (1, 2)]
        for k, piece in enumerate(pieces):
            out_ref[also + k % 2, k // 2] = piece
        return carry

    lax.fori_loop(0, count_ref[1], again, 0)


def pack(caps, count, tiles, place, arrived):
    smem = pl.BlockSpec(memory_space=pltpu.SMEM)
    vmem = pl.BlockSpec(memory_space=pltpu.VMEM)
    return pl.pallas_call(
        partial(pack_kernel, caps),
        in_specs=[smem, smem, smem, vmem],
        out_specs=vmem,
        out_shape=jax.ShapeDtypeStruct(
            (SERVERS * caps[0], MATCH, PIECE, HEAD_SIZE), jnp.bfloat16
        ),
        compiler_params=pltpu.CompilerParams(vmem_limit_bytes=VMEM),
        name="pack_units",
    )(count, tiles, place, arrived)


def unpack_kernel(caps, count_ref, tile_ref, place_ref, in_ref, out_ref):
    def back(unit, head, tiles):
        slot = slab(place_ref[unit], caps[1], 0, 1)
        return [mover(in_ref, (slot, j), out_ref, (tile, head)) for j, tile in enumerate(tiles)]

    move_units(lax.shift_right_logical(count_ref[0], STEP.bit_length() - 1), tile_ref, back)


def unpack(caps, count, tiles, place, results):
    smem = pl.BlockSpec(memory_space=pltpu.SMEM)
    vmem = pl.BlockSpec(memory_space=pltpu.VMEM)
    return pl.pallas_call(
        partial(unpack_kernel, caps),
        in_specs=[smem, smem, smem, vmem],
        out_specs=vmem,
        out_shape=jax.ShapeDtypeStruct((TILES, PER_PLANE, PIECE, HEAD_SIZE), jnp.bfloat16),
        compiler_params=pltpu.CompilerParams(vmem_limit_bytes=VMEM),
        name="unpack_units",
    )(count, tiles, place, results)


def row_key(shape, dim):
    row = lax.broadcasted_iota(jnp.int32, shape, dim)
    piece = row // UNIT_PIECE
    tile = lax.rem(row // PIECE, MATCH)
    return tile * TILE + piece * PIECE + lax.rem(row, PIECE)


def attend_kernel(
    caps, used_ref, table_ref, in_ref, out_ref, peak_ref, total_ref, sum_ref, turned_ref, *score_refs
):
    factor = HEAD_SIZE**-0.5 * 1.4426950408889634

    def rows(which):
        return in_ref[:, which].reshape(ROWS, HEAD_SIZE)

    def turn(unit, carry):
        turned_ref[unit] = rows(2 * unit + 1).T
        return carry

    lax.fori_loop(0, used_ref[1], turn, 0)

    def one_query_unit(slot, carry):
        code = table_ref[slot]
        first = lax.shift_right_logical(code, SCALE.bit_length() - 1)
        earlier = code & (SCALE - 1)
        last = first + earlier
        query = rows(caps[0] - 1 - slot)

        def scores_of(unit):
            return lax.dot_general(
                rows(2 * unit), query, (((1,), (1,)), ((), ())), preferred_element_type=jnp.float32
            )

        def unit_at(step):
            return jnp.where(step == 0, last, jnp.minimum(first + step - 1, last))

        def fold(step, now):
            score_refs[1 - now][...] = scores_of(unit_at(step + 1))
            scores = score_refs[now][...]
            old = peak_ref[...]
            peak = jnp.maximum(old, jnp.max(scores, axis=0, keepdims=True))
            weights = jnp.exp2((scores - peak) * factor)
            keep = jnp.exp2((old - peak) * factor)
            peak_ref[...] = peak
            total_ref[...] = total_ref[...] * keep + jnp.sum(weights, axis=0, keepdims=True)
            sum_ref[...] = sum_ref[...] * keep + jnp.dot(
                turned_ref[unit_at(step)],
                weights.astype(jnp.bfloat16),
                preferred_element_type=jnp.float32,
            )

        visible = row_key((ROWS, 1), 0) <= row_key((1, ROWS), 1)
        score_refs[0][...] = jnp.where(visible, scores_of(last), NEGATIVE)
        peak_ref[...] = jnp.full(peak_ref.shape, NEGATIVE, jnp.float32)
        total_ref[...] = jnp.zeros(total_ref.shape, jnp.float32)
        sum_ref[...] = jnp.zeros(sum_ref.shape, jnp.float32)

        def two(i, carry):
            fold(2 * i, 0)
            fold(2 * i + 1, 1)
            return carry

        lax.fori_loop(0, lax.shift_right_logical(earlier + 1, 1), two, 0)

        @pl.when((earlier & 1) == 0)
        def _():
            fold(earlier, 0)

        result = (sum_ref[...] / total_ref[...]).T.astype(jnp.bfloat16)
        out_ref[:, slot] = result.reshape(SERVERS, UNIT_PIECE, HEAD_SIZE)
        return carry

    lax.fori_loop(0, used_ref[0], one_query_unit, 0)


def attend(caps, used, table, units):
    smem = pl.BlockSpec(memory_space=pltpu.SMEM)
    vmem = pl.BlockSpec(memory_space=pltpu.VMEM)
    return pl.pallas_call(
        partial(attend_kernel, caps),
        in_specs=[smem, smem, vmem],
        out_specs=vmem,
        out_shape=jax.ShapeDtypeStruct((SERVERS, caps[1], UNIT_PIECE, HEAD_SIZE), jnp.bfloat16),
        scratch_shapes=[
            pltpu.VMEM((1, ROWS), jnp.float32),
            pltpu.VMEM((1, ROWS), jnp.float32),
            pltpu.VMEM((HEAD_SIZE, ROWS), jnp.float32),
            pltpu.VMEM((caps[0] // 2, HEAD_SIZE, ROWS), jnp.bfloat16),
            pltpu.VMEM((ROWS, ROWS), jnp.float32),
            pltpu.VMEM((ROWS, ROWS), jnp.float32),
        ],
        compiler_params=pltpu.CompilerParams(vmem_limit_bytes=VMEM),
        name="attend",
    )(used, table, units)


def plan(clusters):
    plane = lax.axis_index("z")
    server = lax.axis_index(PLANE)
    clusters = jnp.pad(clusters.T, ((0, SLOT_HEADS - HEADS), (0, 0)))
    tiles = clusters.reshape(SLOT_HEADS, GROUPS, GROUP_TILES)
    index = jnp.arange(GROUP_TILES, dtype=jnp.int32)
    mine, other = tiles[:, :, :, None], tiles[:, :, None, :]
    ahead = (other < mine) | ((other == mine) & (index[None, :] < index[:, None]))
    place = jnp.sum(ahead, axis=3, dtype=jnp.int32)
    at_place = place[:, :, None, :] == index[:, None]
    unit_cluster = jnp.sum(
        jnp.where(at_place[:, :, ::MATCH], tiles[:, :, None, :], 0), axis=3
    ).reshape(SLOT_HEADS, -1)
    units = unit_cluster.shape[1]
    number = jnp.arange(units, dtype=jnp.int32)
    same = unit_cluster[:, :, None] == unit_cluster[:, None, :]
    size = jnp.sum(same, axis=2, dtype=jnp.int32)
    rank = jnp.sum(same & (number[None, :] < number[:, None]), axis=2, dtype=jnp.int32)
    real = jnp.arange(SLOT_HEADS)[:, None] < HEADS
    cut = jnp.where(size >= SPLIT, size * 7 // 10, 0)
    lead = (rank == 0) & real
    whole = jnp.where(lead, (3 * size - cut) * SCALE + size - cut, 0).reshape(PLANES, UNITS)
    front = jnp.where(lead, 3 * cut * SCALE + cut, 0).reshape(PLANES, UNITS)
    tasks = jnp.concatenate([whole, front], axis=1)
    every = jnp.arange(2 * UNITS, dtype=jnp.int32)
    mine, other = tasks[:, :, None], tasks[:, None, :]
    order = jnp.sum(
        (other > mine) | ((other == mine) & (every[None, :] < every[:, None])),
        axis=2,
        dtype=jnp.int32,
    )
    sizes = jnp.sum(
        jnp.where(order[:, None, :] == every[:UNITS, None], tasks[:, None, :], 0), axis=2
    )
    count = jnp.max(jnp.sum(tasks > 0, axis=1, dtype=jnp.int32)).reshape(1)
    sizes = jnp.broadcast_to(
        sizes.T.astype(jnp.float32)[:, :, None], (UNITS, PLANES, 128)
    )
    key, load = assign(count, sizes)
    load = jnp.where(jnp.arange(128)[None, :] < SERVERS, load, 0.0).astype(jnp.int32)
    most = jnp.max(load // SCALE), jnp.max(load % SCALE)
    key = lax.dynamic_slice(key, (0, plane, 0), (UNITS, 1, 1)).reshape(UNITS).astype(jnp.int32)
    load = lax.dynamic_index_in_dim(load, plane, 0, keepdims=False)
    first = plane * PER_PLANE

    def own(array):
        return lax.dynamic_slice_in_dim(array, first, PER_PLANE, 0)

    own_order = lax.dynamic_index_in_dim(order, plane, 0, keepdims=False)
    own_order = own_order.reshape(2, PER_PLANE, 1, units)
    own_rank, own_cut = own(rank), own(cut)
    leader = own(same) & (own_rank == 0)[:, None, :]
    task = jnp.sum(jnp.where(leader, own_order, 0), axis=3).reshape(2, UNITS)
    code = jnp.sum(
        jnp.where(task[:, :, None] == every[:UNITS], key, 0), axis=2
    )
    own_rank, own_cut = own_rank.reshape(UNITS), own_cut.reshape(UNITS)
    owner, before = code % 128, code // 128
    query_base = before % SCALE
    base = (before // SCALE - query_base) // 2
    own_count = jnp.clip(HEADS - first, 0, PER_PLANE) * units
    live = every[:UNITS] < own_count
    in_front = (own_rank < own_cut) & live
    query_owner = jnp.where(in_front, owner[1], owner[0])
    query_slot = jnp.where(in_front, query_base[1] + own_rank, query_base[0] + own_rank - own_cut)
    earlier = jnp.sum(
        in_front[None, :] & (every[None, :UNITS] < every[:UNITS, None]), axis=1, dtype=jnp.int32
    )
    again = jnp.sum(
        jnp.where(
            in_front[None, :] & (earlier[None, :] == every[:UNITS, None]), every[None, :UNITS], 0
        ),
        axis=1,
    )
    place = jnp.concatenate(
        [
            query_owner * SCALE + query_slot,
            owner[0] * SCALE + base[0] + own_rank,
            owner[1] * SCALE + base[1] + own_rank,
            again,
        ]
    )
    tile_of = own(
        jnp.sum(jnp.where(at_place, index, 0), axis=3, dtype=jnp.int32)
    ) + jnp.arange(GROUPS, dtype=jnp.int32)[:, None] * GROUP_TILES
    here = (
        ((query_owner == server) & live)[None, :]
        & (query_slot[None, :] == jnp.arange(SCALE, dtype=jnp.int32)[:, None])
    )
    table = jnp.where(in_front, base[1], base[0]) * SCALE + own_rank
    table = jnp.sum(jnp.where(here, table[None, :], 0), axis=1)
    mine = jnp.sum(jnp.where(jnp.arange(128) == server, load, 0))
    used = jnp.stack([mine % SCALE, (mine // SCALE - mine % SCALE) // 2])
    counts = jnp.stack([own_count, jnp.sum(in_front, dtype=jnp.int32)])
    return (counts, tile_of.reshape(-1), place, table, used), most


def exchange(caps, arrived, count, tiles, place, table, used):
    packed = pack(caps, count, tiles, place, arrived)
    packed = packed.reshape(SERVERS, -1, UNIT_PIECE, HEAD_SIZE)
    units = lax.all_to_all(packed, PLANE, split_axis=0, concat_axis=0, tiled=True)
    results = attend(caps, used, table, units)
    results = lax.all_to_all(results, PLANE, split_axis=0, concat_axis=0, tiled=True)
    results = results.reshape(SERVERS * caps[1], MATCH, PIECE, HEAD_SIZE)
    return unpack(caps, count, tiles, place, results)


def on_device(queries, keys, values, tile_cluster):
    clusters = jnp.broadcast_to(tile_cluster.reshape(1, 1, HEADS), (TILES, 1, HEADS))
    clusters = lax.all_to_all(clusters, AXES, split_axis=0, concat_axis=0, tiled=True)
    clusters = clusters.reshape(TILES, HEADS)
    stacked = jnp.stack([queries, keys, values], axis=1)
    stacked = jnp.pad(stacked, ((0, SLOT_HEADS - HEADS), (0, 0), (0, 0), (0, 0)))
    stacked = stacked.reshape(PLANES, PER_PLANE, 3, 2, SERVERS // 2, PIECE, HEAD_SIZE)
    outgoing = stacked.transpose(3, 0, 4, 1, 2, 5, 6)
    outgoing = outgoing.reshape(TILES, PER_PLANE * 3, PIECE, HEAD_SIZE)
    arrived = lax.all_to_all(outgoing, AXES, split_axis=0, concat_axis=0, tiled=True)
    tables, (most_slabs, most_queries) = plan(clusters)
    which = jnp.int32(len(CAPACITIES) - 1)
    for i in range(len(CAPACITIES) - 2, -1, -1):
        fits = (most_slabs <= CAPACITIES[i][0]) & (most_queries <= CAPACITIES[i][1])
        which = jnp.where(fits, i, which)
    back = lax.switch(which, [partial(exchange, caps) for caps in CAPACITIES], arrived, *tables)
    back = lax.all_to_all(back, AXES, split_axis=0, concat_axis=0, tiled=True)
    back = back.reshape(2, PLANES, SERVERS // 2, PER_PLANE, PIECE, HEAD_SIZE)
    back = back.transpose(1, 3, 0, 2, 4, 5).reshape(SLOT_HEADS, TILE, HEAD_SIZE)
    return back[:HEADS]


def solution(mesh):
    fine = Mesh(mesh.devices.reshape(SIZES), AXES)
    rows = ("ylo", "z", "yhi", "x", "core")
    return jax.shard_map(
        on_device,
        mesh=fine,
        in_specs=(
            P(None, rows, None),
            P(None, rows, None),
            P(None, rows, None),
            P(None, rows),
        ),
        out_specs=P(None, rows, None),
        check_vma=False,
    )
```

```python
from functools import partial

import jax
import jax.numpy as jnp
from jax import lax
from jax.experimental import pallas as pl
from jax.experimental.pallas import tpu as pltpu
from jax.sharding import Mesh
from jax.sharding import PartitionSpec as P

AXES = ("ylo", "z", "yhi", "x", "core")
PLANE = ("ylo", "yhi", "x", "core")
SIZES = (2, 8, 2, 4, 2)

HEADS = 20
PLANES = 8
PER_PLANE = 3
SLOT_HEADS = PLANES * PER_PLANE
SERVERS = 32
GROUPS = 16
GROUP_TILES = 16
TILES = 256
TILE = 128
MATCH = 4
UNITS = PER_PLANE * GROUPS * GROUP_TILES // MATCH
PIECE = TILE // SERVERS
HEAD_SIZE = 128
CAPACITIES = ((21, 7), (22, 7), (25, 8), (32, 11), (72, 24))
SPLIT = 7
SPLIT_AGAIN = 9
SCALE = 64
STEP = 4
ROWS = MATCH * TILE
UNIT_PIECE = MATCH * PIECE
NEGATIVE = -1e30
VMEM = 56 * 1024 * 1024


def assign_kernel(count_ref, size_ref, key_ref, load_ref):
    lane = lax.broadcasted_iota(jnp.int32, (PLANES, 128), 1)
    lane_number = lane.astype(jnp.float32)
    load_ref[...] = jnp.where(lane < SERVERS, 0.0, 65536.0)

    def step(i, carry):
        load = load_ref[...]
        key = jnp.min(load * 128.0 + lane_number, axis=1, keepdims=True)
        owner = key - jnp.floor(key * (1.0 / 128.0)) * 128.0
        load_ref[...] = load + jnp.where(lane_number == owner, size_ref[i], 0.0)
        key_ref[i] = jnp.broadcast_to(key, (PLANES, 128))
        return carry

    lax.fori_loop(0, count_ref[0], step, 0)


def assign(count, sizes):
    return pl.pallas_call(
        assign_kernel,
        in_specs=[
            pl.BlockSpec(memory_space=pltpu.SMEM),
            pl.BlockSpec(memory_space=pltpu.VMEM),
        ],
        out_specs=[pl.BlockSpec(memory_space=pltpu.VMEM)] * 2,
        out_shape=[
            jax.ShapeDtypeStruct((UNITS, PLANES, 128), jnp.float32),
            jax.ShapeDtypeStruct((PLANES, 128), jnp.float32),
        ],
        compiler_params=pltpu.CompilerParams(vmem_limit_bytes=VMEM),
        name="assign",
    )(count, sizes)


def slab(code, depth, start, width):
    owner = lax.shift_right_logical(code, SCALE.bit_length() - 1)
    return owner * depth + start + (code & (SCALE - 1)) * width


def move_units(steps, tile_ref, move):
    def some(i, carry):
        moves = []
        for k in range(STEP):
            unit = i * STEP + k
            head = lax.shift_right_logical(unit, (UNITS // PER_PLANE).bit_length() - 1)
            moves += move(unit, head, [tile_ref[unit * MATCH + j] for j in range(MATCH)])
        pieces = [load() for load, _ in moves]
        for piece, (_, store) in zip(pieces, moves):
            store(piece)
        return carry

    lax.fori_loop(0, steps, some, 0)


def mover(in_ref, source, out_ref, target):
    def store(piece):
        out_ref[target] = piece

    return lambda: in_ref[source], store


def pack_kernel(caps, count_ref, tile_ref, place_ref, in_ref, out_ref):
    depth = caps[0]

    def first(unit, head, tiles):
        to_query = slab(place_ref[unit], depth, depth - 1, -1)
        to_keys = slab(place_ref[UNITS + unit], depth, 0, 2)
        return [
            mover(in_ref, (tile, head * 3 + s), out_ref, (slot, j))
            for j, tile in enumerate(tiles)
            for s, slot in enumerate((to_query, to_keys, to_keys + 1))
        ]

    move_units(lax.shift_right_logical(count_ref[0], STEP.bit_length() - 1), tile_ref, first)

    def again(i, carry):
        entry = place_ref[4 * UNITS + i]
        unit = jnp.where(entry >= UNITS, entry - UNITS, entry)
        head = lax.shift_right_logical(unit, (UNITS // PER_PLANE).bit_length() - 1)
        also = slab(place_ref[2 * UNITS + entry], depth, 0, 2)
        tiles = [tile_ref[unit * MATCH + j] for j in range(MATCH)]
        pieces = [in_ref[tile, head * 3 + s] for tile in tiles for s in (1, 2)]
        for k, piece in enumerate(pieces):
            out_ref[also + k % 2, k // 2] = piece
        return carry

    lax.fori_loop(0, count_ref[1], again, 0)


def pack(caps, count, tiles, place, arrived):
    smem = pl.BlockSpec(memory_space=pltpu.SMEM)
    vmem = pl.BlockSpec(memory_space=pltpu.VMEM)
    return pl.pallas_call(
        partial(pack_kernel, caps),
        in_specs=[smem, smem, smem, vmem],
        out_specs=vmem,
        out_shape=jax.ShapeDtypeStruct(
            (SERVERS * caps[0], MATCH, PIECE, HEAD_SIZE), jnp.bfloat16
        ),
        compiler_params=pltpu.CompilerParams(vmem_limit_bytes=VMEM),
        name="pack_units",
    )(count, tiles, place, arrived)


def unpack_kernel(caps, count_ref, tile_ref, place_ref, in_ref, out_ref):
    def back(unit, head, tiles):
        slot = slab(place_ref[unit], caps[1], 0, 1)
        return [mover(in_ref, (slot, j), out_ref, (tile, head)) for j, tile in enumerate(tiles)]

    move_units(lax.shift_right_logical(count_ref[0], STEP.bit_length() - 1), tile_ref, back)


def unpack(caps, count, tiles, place, results):
    smem = pl.BlockSpec(memory_space=pltpu.SMEM)
    vmem = pl.BlockSpec(memory_space=pltpu.VMEM)
    return pl.pallas_call(
        partial(unpack_kernel, caps),
        in_specs=[smem, smem, smem, vmem],
        out_specs=vmem,
        out_shape=jax.ShapeDtypeStruct((TILES, PER_PLANE, PIECE, HEAD_SIZE), jnp.bfloat16),
        compiler_params=pltpu.CompilerParams(vmem_limit_bytes=VMEM),
        name="unpack_units",
    )(count, tiles, place, results)


def spread_kernel(*refs):
    out_ref = refs[3]
    half = SERVERS // 2
    for s in range(3):
        for head in range(HEADS):
            plane, slot = divmod(head, PER_PLANE)
            for y in range(2):
                devices = pl.ds((y * PLANES + plane) * half, half)
                out_ref[devices, slot * 3 + s] = refs[s][head, y * half : (y + 1) * half]


def spread(queries, keys, values):
    vmem = pl.BlockSpec(memory_space=pltpu.VMEM)
    pieces = [a.reshape(HEADS, SERVERS, PIECE, HEAD_SIZE) for a in (queries, keys, values)]
    return pl.pallas_call(
        spread_kernel,
        in_specs=[vmem] * 3,
        out_specs=vmem,
        out_shape=jax.ShapeDtypeStruct((TILES, PER_PLANE * 3, PIECE, HEAD_SIZE), jnp.bfloat16),
        compiler_params=pltpu.CompilerParams(vmem_limit_bytes=VMEM),
        name="spread_rows",
    )(*pieces)


def collect_kernel(in_ref, out_ref):
    half = SERVERS // 2
    for head in range(HEADS):
        plane, slot = divmod(head, PER_PLANE)
        for y in range(2):
            devices = pl.ds((y * PLANES + plane) * half, half)
            out_ref[head, y * half : (y + 1) * half] = in_ref[devices, slot]


def collect(back):
    vmem = pl.BlockSpec(memory_space=pltpu.VMEM)
    rows = pl.pallas_call(
        collect_kernel,
        in_specs=[vmem],
        out_specs=vmem,
        out_shape=jax.ShapeDtypeStruct((HEADS, SERVERS, PIECE, HEAD_SIZE), jnp.bfloat16),
        compiler_params=pltpu.CompilerParams(vmem_limit_bytes=VMEM),
        name="collect_rows",
    )(back)
    return rows.reshape(HEADS, TILE, HEAD_SIZE)


def row_key(shape, dim):
    row = lax.broadcasted_iota(jnp.int32, shape, dim)
    piece = row // UNIT_PIECE
    tile = lax.rem(row // PIECE, MATCH)
    return tile * TILE + piece * PIECE + lax.rem(row, PIECE)


def attend_kernel(
    caps, used_ref, table_ref, in_ref, out_ref, peak_ref, total_ref, sum_ref, turned_ref, *score_refs
):
    factor = HEAD_SIZE**-0.5 * 1.4426950408889634

    def rows(which):
        return in_ref[:, which].reshape(ROWS, HEAD_SIZE)

    def turn(unit, carry):
        turned_ref[unit] = rows(2 * unit + 1).T
        return carry

    lax.fori_loop(0, used_ref[1], turn, 0)

    def one_query_unit(slot, carry):
        code = table_ref[slot]
        first = lax.shift_right_logical(code, SCALE.bit_length() - 1)
        earlier = code & (SCALE - 1)
        last = first + earlier
        query = rows(caps[0] - 1 - slot)

        def scores_of(unit):
            return lax.dot_general(
                rows(2 * unit), query, (((1,), (1,)), ((), ())), preferred_element_type=jnp.float32
            )

        def unit_at(step):
            return jnp.where(step == 0, last, jnp.minimum(first + step - 1, last))

        def fold(step, now):
            score_refs[1 - now][...] = scores_of(unit_at(step + 1))
            scores = score_refs[now][...]
            old = peak_ref[...]
            peak = jnp.maximum(old, jnp.max(scores, axis=0, keepdims=True))
            weights = jnp.exp2((scores - peak) * factor)
            keep = jnp.exp2((old - peak) * factor)
            peak_ref[...] = peak
            total_ref[...] = total_ref[...] * keep + jnp.sum(weights, axis=0, keepdims=True)
            sum_ref[...] = sum_ref[...] * keep + jnp.dot(
                turned_ref[unit_at(step)],
                weights.astype(jnp.bfloat16),
                preferred_element_type=jnp.float32,
            )

        visible = row_key((ROWS, 1), 0) <= row_key((1, ROWS), 1)
        score_refs[0][...] = jnp.where(visible, scores_of(last), NEGATIVE)
        peak_ref[...] = jnp.full(peak_ref.shape, NEGATIVE, jnp.float32)
        total_ref[...] = jnp.zeros(total_ref.shape, jnp.float32)
        sum_ref[...] = jnp.zeros(sum_ref.shape, jnp.float32)

        def two(i, carry):
            fold(2 * i, 0)
            fold(2 * i + 1, 1)
            return carry

        lax.fori_loop(0, lax.shift_right_logical(earlier + 1, 1), two, 0)

        @pl.when((earlier & 1) == 0)
        def _():
            fold(earlier, 0)

        result = (sum_ref[...] / total_ref[...]).T.astype(jnp.bfloat16)
        out_ref[:, slot] = result.reshape(SERVERS, UNIT_PIECE, HEAD_SIZE)
        return carry

    lax.fori_loop(0, used_ref[0], one_query_unit, 0)


def attend(caps, used, table, units):
    smem = pl.BlockSpec(memory_space=pltpu.SMEM)
    vmem = pl.BlockSpec(memory_space=pltpu.VMEM)
    return pl.pallas_call(
        partial(attend_kernel, caps),
        in_specs=[smem, smem, vmem],
        out_specs=vmem,
        out_shape=jax.ShapeDtypeStruct((SERVERS, caps[1], UNIT_PIECE, HEAD_SIZE), jnp.bfloat16),
        scratch_shapes=[
            pltpu.VMEM((1, ROWS), jnp.float32),
            pltpu.VMEM((1, ROWS), jnp.float32),
            pltpu.VMEM((HEAD_SIZE, ROWS), jnp.float32),
            pltpu.VMEM((caps[0] // 2, HEAD_SIZE, ROWS), jnp.bfloat16),
            pltpu.VMEM((ROWS, ROWS), jnp.float32),
            pltpu.VMEM((ROWS, ROWS), jnp.float32),
        ],
        compiler_params=pltpu.CompilerParams(vmem_limit_bytes=VMEM),
        name="attend",
    )(used, table, units)


def plan(clusters):
    plane = lax.axis_index("z")
    server = lax.axis_index(PLANE)
    clusters = jnp.pad(clusters.T, ((0, SLOT_HEADS - HEADS), (0, 0)))
    tiles = clusters.reshape(SLOT_HEADS, GROUPS, GROUP_TILES)
    index = jnp.arange(GROUP_TILES, dtype=jnp.int32)
    mine, other = tiles[:, :, :, None], tiles[:, :, None, :]
    ahead = (other < mine) | ((other == mine) & (index[None, :] < index[:, None]))
    place = jnp.sum(ahead, axis=3, dtype=jnp.int32)
    at_place = place[:, :, None, :] == index[:, None]
    unit_cluster = jnp.sum(
        jnp.where(at_place[:, :, ::MATCH], tiles[:, :, None, :], 0), axis=3
    ).reshape(SLOT_HEADS, -1)
    units = unit_cluster.shape[1]
    number = jnp.arange(units, dtype=jnp.int32)
    same = unit_cluster[:, :, None] == unit_cluster[:, None, :]
    size = jnp.sum(same, axis=2, dtype=jnp.int32)
    rank = jnp.sum(same & (number[None, :] < number[:, None]), axis=2, dtype=jnp.int32)
    real = jnp.arange(SLOT_HEADS)[:, None] < HEADS
    again_cut = size >= SPLIT_AGAIN
    cut = jnp.where(again_cut, size * 6 // 10, jnp.where(size >= SPLIT, size * 7 // 10, 0))
    last_cut = jnp.where(again_cut, size * 8 // 10, cut)
    lead = (rank == 0) & real
    number_of_tasks = 3 * UNITS

    def loads(keys, queries):
        load = (2 * keys + queries) * SCALE + queries
        return jnp.where(lead & (queries > 0), load, 0).reshape(PLANES, UNITS)

    tasks = jnp.concatenate(
        [loads(size, size - last_cut), loads(cut, cut), loads(last_cut, last_cut - cut)], axis=1
    )
    every = jnp.arange(number_of_tasks, dtype=jnp.int32)
    mine, other = tasks[:, :, None], tasks[:, None, :]
    order = jnp.sum(
        (other > mine) | ((other == mine) & (every[None, :] < every[:, None])),
        axis=2,
        dtype=jnp.int32,
    )
    sizes = jnp.sum(
        jnp.where(order[:, None, :] == every[:UNITS, None], tasks[:, None, :], 0), axis=2
    )
    count = jnp.max(jnp.sum(tasks > 0, axis=1, dtype=jnp.int32)).reshape(1)
    sizes = jnp.broadcast_to(
        sizes.T.astype(jnp.float32)[:, :, None], (UNITS, PLANES, 128)
    )
    key, load = assign(count, sizes)
    load = jnp.where(jnp.arange(128)[None, :] < SERVERS, load, 0.0).astype(jnp.int32)
    most = jnp.max(load // SCALE), jnp.max(load % SCALE)
    key = lax.dynamic_slice(key, (0, plane, 0), (UNITS, 1, 1)).reshape(UNITS).astype(jnp.int32)
    load = lax.dynamic_index_in_dim(load, plane, 0, keepdims=False)
    first = plane * PER_PLANE

    def own(array):
        return lax.dynamic_slice_in_dim(array, first, PER_PLANE, 0)

    own_order = lax.dynamic_index_in_dim(order, plane, 0, keepdims=False)
    own_order = own_order.reshape(3, PER_PLANE, 1, units)
    own_rank, own_cut, own_last_cut = own(rank), own(cut), own(last_cut)
    leader = own(same) & (own_rank == 0)[:, None, :]
    task = jnp.sum(jnp.where(leader, own_order, 0), axis=3).reshape(3, UNITS)
    code = jnp.sum(
        jnp.where(task[:, :, None] == every[:UNITS], key, 0), axis=2
    )
    own_rank, own_cut = own_rank.reshape(UNITS), own_cut.reshape(UNITS)
    own_last_cut = own_last_cut.reshape(UNITS)
    owner, before = code % 128, code // 128
    query_base = before % SCALE
    base = (before // SCALE - query_base) // 2
    own_count = jnp.clip(HEADS - first, 0, PER_PLANE) * units
    live = every[:UNITS] < own_count
    in_front = (own_rank < own_cut) & live
    in_second = (own_rank < own_last_cut) & (own_last_cut > own_cut) & live

    def of_task(first, second, last):
        return jnp.where(in_front, first, jnp.where(in_second, second, last))

    query_owner = of_task(owner[1], owner[2], owner[0])
    query_slot = own_rank + of_task(
        query_base[1], query_base[2] - own_cut, query_base[0] - own_last_cut
    )
    copied = jnp.concatenate([in_front, in_second])
    entries = every[: 2 * UNITS]
    earlier = jnp.sum(
        copied[None, :] & (entries[None, :] < entries[:, None]), axis=1, dtype=jnp.int32
    )
    again = jnp.sum(
        jnp.where(copied[None, :] & (earlier[None, :] == entries[:, None]), entries[None, :], 0),
        axis=1,
    )
    place = jnp.concatenate(
        [query_owner * SCALE + query_slot]
        + [owner[i] * SCALE + base[i] + own_rank for i in range(3)]
        + [again]
    )
    tile_of = own(
        jnp.sum(jnp.where(at_place, index, 0), axis=3, dtype=jnp.int32)
    ) + jnp.arange(GROUPS, dtype=jnp.int32)[:, None] * GROUP_TILES
    here = (
        ((query_owner == server) & live)[None, :]
        & (query_slot[None, :] == jnp.arange(SCALE, dtype=jnp.int32)[:, None])
    )
    table = of_task(base[1], base[2], base[0]) * SCALE + own_rank
    table = jnp.sum(jnp.where(here, table[None, :], 0), axis=1)
    mine = jnp.sum(jnp.where(jnp.arange(128) == server, load, 0))
    used = jnp.stack([mine % SCALE, (mine // SCALE - mine % SCALE) // 2])
    counts = jnp.stack([own_count, jnp.sum(copied, dtype=jnp.int32)])
    return (counts, tile_of.reshape(-1), place, table, used), most


def exchange(caps, arrived, count, tiles, place, table, used):
    packed = pack(caps, count, tiles, place, arrived)
    packed = packed.reshape(SERVERS, -1, UNIT_PIECE, HEAD_SIZE)
    units = lax.all_to_all(packed, PLANE, split_axis=0, concat_axis=0, tiled=True)
    results = attend(caps, used, table, units)
    results = lax.all_to_all(results, PLANE, split_axis=0, concat_axis=0, tiled=True)
    results = results.reshape(SERVERS * caps[1], MATCH, PIECE, HEAD_SIZE)
    return unpack(caps, count, tiles, place, results)


def on_device(queries, keys, values, tile_cluster):
    clusters = jnp.broadcast_to(tile_cluster.reshape(1, 1, HEADS), (TILES, 1, HEADS))
    clusters = lax.all_to_all(clusters, AXES, split_axis=0, concat_axis=0, tiled=True)
    clusters = clusters.reshape(TILES, HEADS)
    outgoing = spread(queries, keys, values)
    arrived = lax.all_to_all(outgoing, AXES, split_axis=0, concat_axis=0, tiled=True)
    tables, (most_slabs, most_queries) = plan(clusters)
    which = jnp.int32(len(CAPACITIES) - 1)
    for i in range(len(CAPACITIES) - 2, -1, -1):
        fits = (most_slabs <= CAPACITIES[i][0]) & (most_queries <= CAPACITIES[i][1])
        which = jnp.where(fits, i, which)
    back = lax.switch(which, [partial(exchange, caps) for caps in CAPACITIES], arrived, *tables)
    back = lax.all_to_all(back, AXES, split_axis=0, concat_axis=0, tiled=True)
    return collect(back)


def solution(mesh):
    fine = Mesh(mesh.devices.reshape(SIZES), AXES)
    rows = ("ylo", "z", "yhi", "x", "core")
    return jax.shard_map(
        on_device,
        mesh=fine,
        in_specs=(
            P(None, rows, None),
            P(None, rows, None),
            P(None, rows, None),
            P(None, rows),
        ),
        out_specs=P(None, rows, None),
        check_vma=False,
    )
```

```python
from functools import partial

import jax
import jax.numpy as jnp
from jax import lax
from jax.experimental import pallas as pl
from jax.experimental.pallas import tpu as pltpu
from jax.sharding import Mesh
from jax.sharding import PartitionSpec as P

AXES = ("ylo", "z", "yhi", "x", "core")
PLANE = ("ylo", "yhi", "x", "core")
SIZES = (2, 8, 2, 4, 2)

HEADS = 20
PLANES = 8
PER_PLANE = 3
SLOT_HEADS = PLANES * PER_PLANE
SERVERS = 32
GROUPS = 16
GROUP_TILES = 16
TILES = 256
TILE = 128
MATCH = 4
UNITS = PER_PLANE * GROUPS * GROUP_TILES // MATCH
PIECE = TILE // SERVERS
HEAD_SIZE = 128
CAPACITIES = ((21, 7), (22, 7), (25, 8), (32, 11), (72, 24))
SPLIT = 7
SPLIT_AGAIN = 9
SCALE = 64
STEP = 8
ROWS = MATCH * TILE
UNIT_PIECE = MATCH * PIECE
NEGATIVE = -1e30
VMEM = 56 * 1024 * 1024


def assign_kernel(count_ref, size_ref, key_ref, load_ref):
    lane = lax.broadcasted_iota(jnp.int32, (PLANES, 128), 1)
    lane_number = lane.astype(jnp.float32)
    load_ref[...] = jnp.where(lane < SERVERS, 0.0, 65536.0)

    def step(i, carry):
        load = load_ref[...]
        key = jnp.min(load * 128.0 + lane_number, axis=1, keepdims=True)
        owner = key - jnp.floor(key * (1.0 / 128.0)) * 128.0
        load_ref[...] = load + jnp.where(lane_number == owner, size_ref[i], 0.0)
        key_ref[i] = jnp.broadcast_to(key, (PLANES, 128))
        return carry

    lax.fori_loop(0, count_ref[0], step, 0)


def assign(count, sizes):
    return pl.pallas_call(
        assign_kernel,
        in_specs=[
            pl.BlockSpec(memory_space=pltpu.SMEM),
            pl.BlockSpec(memory_space=pltpu.VMEM),
        ],
        out_specs=[pl.BlockSpec(memory_space=pltpu.VMEM)] * 2,
        out_shape=[
            jax.ShapeDtypeStruct((UNITS, PLANES, 128), jnp.float32),
            jax.ShapeDtypeStruct((PLANES, 128), jnp.float32),
        ],
        compiler_params=pltpu.CompilerParams(vmem_limit_bytes=VMEM),
        name="assign",
    )(count, sizes)


def slab(code, depth, start, width):
    owner = lax.shift_right_logical(code, SCALE.bit_length() - 1)
    return owner * depth + start + (code & (SCALE - 1)) * width


def move_units(steps, tile_ref, move):
    def some(i, carry):
        moves = []
        for k in range(STEP):
            unit = i * STEP + k
            moves += move(unit, [tile_ref[unit * MATCH + j] for j in range(MATCH)])
        pieces = [load() for load, _ in moves]
        for piece, (_, store) in zip(pieces, moves):
            store(piece)
        return carry

    lax.fori_loop(0, steps, some, 0)


def mover(in_ref, source, out_ref, target):
    def store(piece):
        out_ref[target] = piece

    return lambda: in_ref[source], store


def pack_kernel(caps, count_ref, tile_ref, place_ref, in_ref, out_ref):
    depth = caps[0]

    def first(unit, tiles):
        to_query = slab(place_ref[unit], depth, depth - 1, -1) * MATCH
        to_keys = slab(place_ref[UNITS + unit], depth, 0, 2) * MATCH
        return [
            mover(in_ref, tile * 3 + s, out_ref, slot + j)
            for j, tile in enumerate(tiles)
            for s, slot in enumerate((to_query, to_keys, to_keys + MATCH))
        ]

    move_units(lax.shift_right_logical(count_ref[0], STEP.bit_length() - 1), tile_ref, first)

    def again(i, carry):
        entry = place_ref[4 * UNITS + i]
        unit = jnp.where(entry >= UNITS, entry - UNITS, entry)
        also = slab(place_ref[2 * UNITS + entry], depth, 0, 2) * MATCH
        tiles = [tile_ref[unit * MATCH + j] for j in range(MATCH)]
        pieces = [in_ref[tile * 3 + s] for s in (1, 2) for tile in tiles]
        for k, piece in enumerate(pieces):
            out_ref[also + k] = piece
        return carry

    lax.fori_loop(0, count_ref[1], again, 0)


def pack(caps, count, tiles, place, arrived):
    smem = pl.BlockSpec(memory_space=pltpu.SMEM)
    vmem = pl.BlockSpec(memory_space=pltpu.VMEM)
    return pl.pallas_call(
        partial(pack_kernel, caps),
        in_specs=[smem, smem, smem, vmem],
        out_specs=vmem,
        out_shape=jax.ShapeDtypeStruct(
            (SERVERS * caps[0] * MATCH, PIECE, HEAD_SIZE), jnp.bfloat16
        ),
        compiler_params=pltpu.CompilerParams(vmem_limit_bytes=VMEM),
        name="pack_units",
    )(count, tiles, place, arrived)


def unpack_kernel(caps, count_ref, tile_ref, place_ref, in_ref, out_ref):
    out_ref = out_ref.reshape(TILES * PER_PLANE, PIECE, HEAD_SIZE)

    def back(unit, tiles):
        slot = slab(place_ref[unit], caps[1], 0, 1) * MATCH
        return [mover(in_ref, slot + j, out_ref, tile) for j, tile in enumerate(tiles)]

    move_units(lax.shift_right_logical(count_ref[0], STEP.bit_length() - 1), tile_ref, back)


def unpack(caps, count, tiles, place, results):
    smem = pl.BlockSpec(memory_space=pltpu.SMEM)
    vmem = pl.BlockSpec(memory_space=pltpu.VMEM)
    return pl.pallas_call(
        partial(unpack_kernel, caps),
        in_specs=[smem, smem, smem, vmem],
        out_specs=vmem,
        out_shape=jax.ShapeDtypeStruct((TILES, PER_PLANE, PIECE, HEAD_SIZE), jnp.bfloat16),
        compiler_params=pltpu.CompilerParams(vmem_limit_bytes=VMEM),
        name="unpack_units",
    )(count, tiles, place, results)


def spread_kernel(*refs):
    out_ref = refs[3]
    half = SERVERS // 2
    for s in range(3):
        for head in range(HEADS):
            plane, slot = divmod(head, PER_PLANE)
            for y in range(2):
                devices = pl.ds((y * PLANES + plane) * half, half)
                out_ref[devices, slot * 3 + s] = refs[s][head, y * half : (y + 1) * half]


def spread(queries, keys, values):
    vmem = pl.BlockSpec(memory_space=pltpu.VMEM)
    pieces = [a.reshape(HEADS, SERVERS, PIECE, HEAD_SIZE) for a in (queries, keys, values)]
    return pl.pallas_call(
        spread_kernel,
        in_specs=[vmem] * 3,
        out_specs=vmem,
        out_shape=jax.ShapeDtypeStruct((TILES, PER_PLANE * 3, PIECE, HEAD_SIZE), jnp.bfloat16),
        compiler_params=pltpu.CompilerParams(vmem_limit_bytes=VMEM),
        name="spread_rows",
    )(*pieces)


def row_key(shape, dim):
    row = lax.broadcasted_iota(jnp.int32, shape, dim)
    piece = row // UNIT_PIECE
    tile = lax.rem(row // PIECE, MATCH)
    return tile * TILE + piece * PIECE + lax.rem(row, PIECE)


def attend_kernel(
    caps, used_ref, table_ref, in_ref, out_ref, peak_ref, total_ref, sum_ref, turned_ref, *score_refs
):
    factor = HEAD_SIZE**-0.5 * 1.4426950408889634

    def rows(which):
        return in_ref[:, which].reshape(ROWS, HEAD_SIZE)

    def turn(unit, carry):
        turned_ref[unit] = rows(2 * unit + 1).T
        return carry

    lax.fori_loop(0, used_ref[1], turn, 0)

    def one_query_unit(slot, carry):
        code = table_ref[slot]
        first = lax.shift_right_logical(code, SCALE.bit_length() - 1)
        earlier = code & (SCALE - 1)
        last = first + earlier
        query = rows(caps[0] - 1 - slot)

        def scores_of(unit):
            return lax.dot_general(
                rows(2 * unit), query, (((1,), (1,)), ((), ())), preferred_element_type=jnp.float32
            )

        def unit_at(step):
            return jnp.where(step == 0, last, jnp.minimum(first + step - 1, last))

        def fold(step, now):
            score_refs[1 - now][...] = scores_of(unit_at(step + 1))
            scores = score_refs[now][...]
            old = peak_ref[...]
            peak = jnp.maximum(old, jnp.max(scores, axis=0, keepdims=True))
            weights = jnp.exp2((scores - peak) * factor)
            keep = jnp.exp2((old - peak) * factor)
            peak_ref[...] = peak
            total_ref[...] = total_ref[...] * keep + jnp.sum(weights, axis=0, keepdims=True)
            sum_ref[...] = sum_ref[...] * keep + jnp.dot(
                turned_ref[unit_at(step)],
                weights.astype(jnp.bfloat16),
                preferred_element_type=jnp.float32,
            )

        visible = row_key((ROWS, 1), 0) <= row_key((1, ROWS), 1)
        score_refs[0][...] = jnp.where(visible, scores_of(last), NEGATIVE)
        peak_ref[...] = jnp.full(peak_ref.shape, NEGATIVE, jnp.float32)
        total_ref[...] = jnp.zeros(total_ref.shape, jnp.float32)
        sum_ref[...] = jnp.zeros(sum_ref.shape, jnp.float32)

        def two(i, carry):
            fold(2 * i, 0)
            fold(2 * i + 1, 1)
            return carry

        lax.fori_loop(0, lax.shift_right_logical(earlier + 1, 1), two, 0)

        @pl.when((earlier & 1) == 0)
        def _():
            fold(earlier, 0)

        result = (sum_ref[...] / total_ref[...]).T.astype(jnp.bfloat16)
        out_ref[:, slot] = result.reshape(SERVERS, UNIT_PIECE, HEAD_SIZE)
        return carry

    lax.fori_loop(0, used_ref[0], one_query_unit, 0)


def attend(caps, used, table, units):
    smem = pl.BlockSpec(memory_space=pltpu.SMEM)
    vmem = pl.BlockSpec(memory_space=pltpu.VMEM)
    return pl.pallas_call(
        partial(attend_kernel, caps),
        in_specs=[smem, smem, vmem],
        out_specs=vmem,
        out_shape=jax.ShapeDtypeStruct((SERVERS, caps[1], UNIT_PIECE, HEAD_SIZE), jnp.bfloat16),
        scratch_shapes=[
            pltpu.VMEM((1, ROWS), jnp.float32),
            pltpu.VMEM((1, ROWS), jnp.float32),
            pltpu.VMEM((HEAD_SIZE, ROWS), jnp.float32),
            pltpu.VMEM((caps[0] // 2, HEAD_SIZE, ROWS), jnp.bfloat16),
            pltpu.VMEM((ROWS, ROWS), jnp.float32),
            pltpu.VMEM((ROWS, ROWS), jnp.float32),
        ],
        compiler_params=pltpu.CompilerParams(vmem_limit_bytes=VMEM),
        name="attend",
    )(used, table, units)


def plan(clusters):
    plane = lax.axis_index("z")
    server = lax.axis_index(PLANE)
    clusters = jnp.pad(clusters.T, ((0, SLOT_HEADS - HEADS), (0, 0)))
    tiles = clusters.reshape(SLOT_HEADS, GROUPS, GROUP_TILES)
    index = jnp.arange(GROUP_TILES, dtype=jnp.int32)
    mine, other = tiles[:, :, :, None], tiles[:, :, None, :]
    ahead = (other < mine) | ((other == mine) & (index[None, :] < index[:, None]))
    place = jnp.sum(ahead, axis=3, dtype=jnp.int32)
    at_place = place[:, :, None, :] == index[:, None]
    unit_cluster = jnp.sum(
        jnp.where(at_place[:, :, ::MATCH], tiles[:, :, None, :], 0), axis=3
    ).reshape(SLOT_HEADS, -1)
    units = unit_cluster.shape[1]
    number = jnp.arange(units, dtype=jnp.int32)
    same = unit_cluster[:, :, None] == unit_cluster[:, None, :]
    size = jnp.sum(same, axis=2, dtype=jnp.int32)
    rank = jnp.sum(same & (number[None, :] < number[:, None]), axis=2, dtype=jnp.int32)
    real = jnp.arange(SLOT_HEADS)[:, None] < HEADS
    again_cut = size >= SPLIT_AGAIN
    cut = jnp.where(again_cut, size * 6 // 10, jnp.where(size >= SPLIT, size * 7 // 10, 0))
    last_cut = jnp.where(again_cut, size * 8 // 10, cut)
    lead = (rank == 0) & real
    number_of_tasks = 3 * UNITS

    def loads(keys, queries):
        load = (2 * keys + queries) * SCALE + queries
        return jnp.where(lead & (queries > 0), load, 0).reshape(PLANES, UNITS)

    tasks = jnp.concatenate(
        [loads(size, size - last_cut), loads(cut, cut), loads(last_cut, last_cut - cut)], axis=1
    )
    every = jnp.arange(number_of_tasks, dtype=jnp.int32)
    mine, other = tasks[:, :, None], tasks[:, None, :]
    order = jnp.sum(
        (other > mine) | ((other == mine) & (every[None, :] < every[:, None])),
        axis=2,
        dtype=jnp.int32,
    )
    sizes = jnp.sum(
        jnp.where(order[:, None, :] == every[:UNITS, None], tasks[:, None, :], 0), axis=2
    )
    count = jnp.max(jnp.sum(tasks > 0, axis=1, dtype=jnp.int32)).reshape(1)
    sizes = jnp.broadcast_to(
        sizes.T.astype(jnp.float32)[:, :, None], (UNITS, PLANES, 128)
    )
    key, load = assign(count, sizes)
    load = jnp.where(jnp.arange(128)[None, :] < SERVERS, load, 0.0).astype(jnp.int32)
    most = jnp.max(load // SCALE), jnp.max(load % SCALE)
    key = lax.dynamic_slice(key, (0, plane, 0), (UNITS, 1, 1)).reshape(UNITS).astype(jnp.int32)
    load = lax.dynamic_index_in_dim(load, plane, 0, keepdims=False)
    first = plane * PER_PLANE

    def own(array):
        return lax.dynamic_slice_in_dim(array, first, PER_PLANE, 0)

    own_order = lax.dynamic_index_in_dim(order, plane, 0, keepdims=False)
    own_order = own_order.reshape(3, PER_PLANE, 1, units)
    own_rank, own_cut, own_last_cut = own(rank), own(cut), own(last_cut)
    leader = own(same) & (own_rank == 0)[:, None, :]
    task = jnp.sum(jnp.where(leader, own_order, 0), axis=3).reshape(3, UNITS)
    code = jnp.sum(
        jnp.where(task[:, :, None] == every[:UNITS], key, 0), axis=2
    )
    own_rank, own_cut = own_rank.reshape(UNITS), own_cut.reshape(UNITS)
    own_last_cut = own_last_cut.reshape(UNITS)
    owner, before = code % 128, code // 128
    query_base = before % SCALE
    base = (before // SCALE - query_base) // 2
    own_count = jnp.clip(HEADS - first, 0, PER_PLANE) * units
    live = every[:UNITS] < own_count
    in_front = (own_rank < own_cut) & live
    in_second = (own_rank < own_last_cut) & (own_last_cut > own_cut) & live

    def of_task(first, second, last):
        return jnp.where(in_front, first, jnp.where(in_second, second, last))

    query_owner = of_task(owner[1], owner[2], owner[0])
    query_slot = own_rank + of_task(
        query_base[1], query_base[2] - own_cut, query_base[0] - own_last_cut
    )
    copied = jnp.concatenate([in_front, in_second])
    entries = every[: 2 * UNITS]
    earlier = jnp.sum(
        copied[None, :] & (entries[None, :] < entries[:, None]), axis=1, dtype=jnp.int32
    )
    again = jnp.sum(
        jnp.where(copied[None, :] & (earlier[None, :] == entries[:, None]), entries[None, :], 0),
        axis=1,
    )
    place = jnp.concatenate(
        [query_owner * SCALE + query_slot]
        + [owner[i] * SCALE + base[i] + own_rank for i in range(3)]
        + [again]
    )
    tile_of = own(
        jnp.sum(jnp.where(at_place, index, 0), axis=3, dtype=jnp.int32)
    ) + jnp.arange(GROUPS, dtype=jnp.int32)[:, None] * GROUP_TILES
    here = (
        ((query_owner == server) & live)[None, :]
        & (query_slot[None, :] == jnp.arange(SCALE, dtype=jnp.int32)[:, None])
    )
    table = of_task(base[1], base[2], base[0]) * SCALE + own_rank
    table = jnp.sum(jnp.where(here, table[None, :], 0), axis=1)
    mine = jnp.sum(jnp.where(jnp.arange(128) == server, load, 0))
    used = jnp.stack([mine % SCALE, (mine // SCALE - mine % SCALE) // 2])
    counts = jnp.stack([own_count, jnp.sum(copied, dtype=jnp.int32)])
    tile_of = tile_of * PER_PLANE + jnp.arange(PER_PLANE, dtype=jnp.int32)[:, None, None]
    return (counts, tile_of.reshape(-1), place, table, used), most


def exchange(caps, arrived, count, tiles, place, table, used):
    pieces = arrived.reshape(-1, PIECE, HEAD_SIZE)
    packed = pack(caps, count, tiles, place, pieces)
    packed = packed.reshape(SERVERS, -1, UNIT_PIECE, HEAD_SIZE)
    units = lax.all_to_all(packed, PLANE, split_axis=0, concat_axis=0, tiled=True)
    results = attend(caps, used, table, units)
    results = lax.all_to_all(results, PLANE, split_axis=0, concat_axis=0, tiled=True)
    results = results.reshape(SERVERS * caps[1] * MATCH, PIECE, HEAD_SIZE)
    return unpack(caps, count, tiles, place, results)


def on_device(queries, keys, values, tile_cluster):
    clusters = jnp.broadcast_to(tile_cluster.reshape(1, 1, HEADS), (TILES, 1, HEADS))
    clusters = lax.all_to_all(clusters, AXES, split_axis=0, concat_axis=0, tiled=True)
    clusters = clusters.reshape(TILES, HEADS)
    outgoing = spread(queries, keys, values)
    arrived = lax.all_to_all(outgoing, AXES, split_axis=0, concat_axis=0, tiled=True)
    tables, (most_slabs, most_queries) = plan(clusters)
    which = jnp.int32(len(CAPACITIES) - 1)
    for i in range(len(CAPACITIES) - 2, -1, -1):
        fits = (most_slabs <= CAPACITIES[i][0]) & (most_queries <= CAPACITIES[i][1])
        which = jnp.where(fits, i, which)
    back = lax.switch(which, [partial(exchange, caps) for caps in CAPACITIES], arrived, *tables)
    back = lax.all_to_all(back, AXES, split_axis=0, concat_axis=0, tiled=True)
    back = back.reshape(2, PLANES, SERVERS // 2, PER_PLANE, PIECE, HEAD_SIZE)
    back = back.transpose(1, 3, 0, 2, 4, 5).reshape(SLOT_HEADS, TILE, HEAD_SIZE)
    return back[:HEADS]


def solution(mesh):
    fine = Mesh(mesh.devices.reshape(SIZES), AXES)
    rows = ("ylo", "z", "yhi", "x", "core")
    return jax.shard_map(
        on_device,
        mesh=fine,
        in_specs=(
            P(None, rows, None),
            P(None, rows, None),
            P(None, rows, None),
            P(None, rows),
        ),
        out_specs=P(None, rows, None),
        check_vma=False,
    )
```

```python
from functools import partial

import jax
import jax.numpy as jnp
from jax import lax
from jax.experimental import pallas as pl
from jax.experimental.pallas import tpu as pltpu
from jax.sharding import Mesh
from jax.sharding import PartitionSpec as P

AXES = ("ylo", "z", "yhi", "x", "core")
PLANE = ("ylo", "yhi", "x", "core")
SIZES = (2, 8, 2, 4, 2)

HEADS = 20
PLANES = 8
PER_PLANE = 3
SLOT_HEADS = PLANES * PER_PLANE
SERVERS = 32
GROUPS = 16
GROUP_TILES = 16
TILES = 256
TILE = 128
MATCH = 4
UNITS = PER_PLANE * GROUPS * GROUP_TILES // MATCH
PIECE = TILE // SERVERS
HEAD_SIZE = 128
CAPACITIES = ((21, 7), (23, 7), (26, 8), (32, 11), (72, 24))
SPLIT = 7
SPLIT_AGAIN = 9
SCALE = 64
STEP = 8
ROWS = MATCH * TILE
UNIT_PIECE = MATCH * PIECE
NEGATIVE = -1e30
VMEM = 56 * 1024 * 1024


def assign_kernel(count_ref, size_ref, key_ref, load_ref):
    lane = lax.broadcasted_iota(jnp.int32, (PLANES, 128), 1)
    lane_number = lane.astype(jnp.float32)
    load_ref[...] = jnp.where(lane < SERVERS, 0.0, 65536.0)

    def step(i, carry):
        load = load_ref[...]
        key = jnp.min(load * 128.0 + lane_number, axis=1, keepdims=True)
        owner = key - jnp.floor(key * (1.0 / 128.0)) * 128.0
        load_ref[...] = load + jnp.where(lane_number == owner, size_ref[i], 0.0)
        key_ref[i] = jnp.broadcast_to(key, (PLANES, 128))
        return carry

    lax.fori_loop(0, count_ref[0], step, 0)


def assign(count, sizes):
    return pl.pallas_call(
        assign_kernel,
        in_specs=[
            pl.BlockSpec(memory_space=pltpu.SMEM),
            pl.BlockSpec(memory_space=pltpu.VMEM),
        ],
        out_specs=[pl.BlockSpec(memory_space=pltpu.VMEM)] * 2,
        out_shape=[
            jax.ShapeDtypeStruct((UNITS, PLANES, 128), jnp.float32),
            jax.ShapeDtypeStruct((PLANES, 128), jnp.float32),
        ],
        compiler_params=pltpu.CompilerParams(vmem_limit_bytes=VMEM),
        name="assign",
    )(count, sizes)


def slab(code, depth, start, width):
    owner = lax.shift_right_logical(code, SCALE.bit_length() - 1)
    return owner * depth + start + (code & (SCALE - 1)) * width


def move_units(steps, tile_ref, move):
    def some(i, carry):
        moves = []
        for k in range(STEP):
            unit = i * STEP + k
            moves += move(unit, [tile_ref[unit * MATCH + j] for j in range(MATCH)])
        pieces = [load() for load, _ in moves]
        for piece, (_, store) in zip(pieces, moves):
            store(piece)
        return carry

    lax.fori_loop(0, steps, some, 0)


def mover(in_ref, source, out_ref, target):
    def store(piece):
        out_ref[target] = piece

    return lambda: in_ref[source], store


def pack_kernel(caps, count_ref, tile_ref, place_ref, in_ref, out_ref):
    depth = caps[0]

    def first(unit, tiles):
        to_query = slab(place_ref[unit], depth, depth - 1, -1) * MATCH
        to_keys = slab(place_ref[UNITS + unit], depth, 0, 2) * MATCH
        return [
            mover(in_ref, tile * 3 + s, out_ref, slot + j)
            for j, tile in enumerate(tiles)
            for s, slot in enumerate((to_query, to_keys, to_keys + MATCH))
        ]

    move_units(lax.shift_right_logical(count_ref[0], STEP.bit_length() - 1), tile_ref, first)

    def again(i, carry):
        entry = place_ref[4 * UNITS + i]
        unit = jnp.where(entry >= UNITS, entry - UNITS, entry)
        also = slab(place_ref[2 * UNITS + entry], depth, 0, 2) * MATCH
        tiles = [tile_ref[unit * MATCH + j] for j in range(MATCH)]
        pieces = [in_ref[tile * 3 + s] for s in (1, 2) for tile in tiles]
        for k, piece in enumerate(pieces):
            out_ref[also + k] = piece
        return carry

    lax.fori_loop(0, count_ref[1], again, 0)


def pack(caps, count, tiles, place, arrived):
    smem = pl.BlockSpec(memory_space=pltpu.SMEM)
    vmem = pl.BlockSpec(memory_space=pltpu.VMEM)
    return pl.pallas_call(
        partial(pack_kernel, caps),
        in_specs=[smem, smem, smem, vmem],
        out_specs=vmem,
        out_shape=jax.ShapeDtypeStruct(
            (SERVERS * caps[0] * MATCH, PIECE, HEAD_SIZE), jnp.bfloat16
        ),
        compiler_params=pltpu.CompilerParams(vmem_limit_bytes=VMEM),
        name="pack_units",
    )(count, tiles, place, arrived)


def unpack_kernel(caps, count_ref, tile_ref, place_ref, in_ref, out_ref):
    out_ref = out_ref.reshape(TILES * PER_PLANE, PIECE, HEAD_SIZE)

    def back(unit, tiles):
        slot = slab(place_ref[unit], caps[1], 0, 1) * MATCH
        return [mover(in_ref, slot + j, out_ref, tile) for j, tile in enumerate(tiles)]

    move_units(lax.shift_right_logical(count_ref[0], STEP.bit_length() - 1), tile_ref, back)


def unpack(caps, count, tiles, place, results):
    smem = pl.BlockSpec(memory_space=pltpu.SMEM)
    vmem = pl.BlockSpec(memory_space=pltpu.VMEM)
    return pl.pallas_call(
        partial(unpack_kernel, caps),
        in_specs=[smem, smem, smem, vmem],
        out_specs=vmem,
        out_shape=jax.ShapeDtypeStruct((TILES, PER_PLANE, PIECE, HEAD_SIZE), jnp.bfloat16),
        compiler_params=pltpu.CompilerParams(vmem_limit_bytes=VMEM),
        name="unpack_units",
    )(count, tiles, place, results)


def spread_kernel(*refs):
    out_ref = refs[3]
    half = SERVERS // 2
    for s in range(3):
        for head in range(HEADS):
            plane, slot = divmod(head, PER_PLANE)
            for y in range(2):
                devices = pl.ds((y * PLANES + plane) * half, half)
                out_ref[devices, slot * 3 + s] = refs[s][head, y * half : (y + 1) * half]


def spread(queries, keys, values):
    vmem = pl.BlockSpec(memory_space=pltpu.VMEM)
    pieces = [a.reshape(HEADS, SERVERS, PIECE, HEAD_SIZE) for a in (queries, keys, values)]
    return pl.pallas_call(
        spread_kernel,
        in_specs=[vmem] * 3,
        out_specs=vmem,
        out_shape=jax.ShapeDtypeStruct((TILES, PER_PLANE * 3, PIECE, HEAD_SIZE), jnp.bfloat16),
        compiler_params=pltpu.CompilerParams(vmem_limit_bytes=VMEM),
        name="spread_rows",
    )(*pieces)


def row_key(shape, dim):
    row = lax.broadcasted_iota(jnp.int32, shape, dim)
    piece = row // UNIT_PIECE
    tile = lax.rem(row // PIECE, MATCH)
    return tile * TILE + piece * PIECE + lax.rem(row, PIECE)


def attend_kernel(
    caps, used_ref, table_ref, in_ref, out_ref, peak_ref, total_ref, sum_ref, turned_ref, *score_refs
):
    factor = HEAD_SIZE**-0.5 * 1.4426950408889634

    def rows(which):
        return in_ref[:, which].reshape(ROWS, HEAD_SIZE)

    def turn(unit, carry):
        turned_ref[unit] = rows(2 * unit + 1).T
        return carry

    lax.fori_loop(0, used_ref[1], turn, 0)

    def one_query_unit(slot, carry):
        code = table_ref[slot]
        first = lax.shift_right_logical(code, SCALE.bit_length() - 1)
        earlier = code & (SCALE - 1)
        last = first + earlier
        query = rows(caps[0] - 1 - slot)

        def scores_of(unit):
            return lax.dot_general(
                rows(2 * unit), query, (((1,), (1,)), ((), ())), preferred_element_type=jnp.float32
            )

        def unit_at(step):
            return jnp.where(step == 0, last, jnp.minimum(first + step - 1, last))

        def fold(step, now):
            score_refs[1 - now][...] = scores_of(unit_at(step + 1))
            scores = score_refs[now][...]
            old = peak_ref[...]
            peak = jnp.maximum(old, jnp.max(scores, axis=0, keepdims=True))
            weights = jnp.exp2((scores - peak) * factor)
            keep = jnp.exp2((old - peak) * factor)
            peak_ref[...] = peak
            total_ref[...] = total_ref[...] * keep + jnp.sum(weights, axis=0, keepdims=True)
            sum_ref[...] = sum_ref[...] * keep + jnp.dot(
                turned_ref[unit_at(step)],
                weights.astype(jnp.bfloat16),
                preferred_element_type=jnp.float32,
            )

        visible = row_key((ROWS, 1), 0) <= row_key((1, ROWS), 1)
        score_refs[0][...] = jnp.where(visible, scores_of(last), NEGATIVE)
        peak_ref[...] = jnp.full(peak_ref.shape, NEGATIVE, jnp.float32)
        total_ref[...] = jnp.zeros(total_ref.shape, jnp.float32)
        sum_ref[...] = jnp.zeros(sum_ref.shape, jnp.float32)

        def two(i, carry):
            fold(2 * i, 0)
            fold(2 * i + 1, 1)
            return carry

        lax.fori_loop(0, lax.shift_right_logical(earlier + 1, 1), two, 0)

        @pl.when((earlier & 1) == 0)
        def _():
            fold(earlier, 0)

        result = (sum_ref[...] / total_ref[...]).T.astype(jnp.bfloat16)
        out_ref[:, slot] = result.reshape(SERVERS, UNIT_PIECE, HEAD_SIZE)
        return carry

    lax.fori_loop(0, used_ref[0], one_query_unit, 0)


def attend(caps, used, table, units):
    smem = pl.BlockSpec(memory_space=pltpu.SMEM)
    vmem = pl.BlockSpec(memory_space=pltpu.VMEM)
    return pl.pallas_call(
        partial(attend_kernel, caps),
        in_specs=[smem, smem, vmem],
        out_specs=vmem,
        out_shape=jax.ShapeDtypeStruct((SERVERS, caps[1], UNIT_PIECE, HEAD_SIZE), jnp.bfloat16),
        scratch_shapes=[
            pltpu.VMEM((1, ROWS), jnp.float32),
            pltpu.VMEM((1, ROWS), jnp.float32),
            pltpu.VMEM((HEAD_SIZE, ROWS), jnp.float32),
            pltpu.VMEM((caps[0] // 2, HEAD_SIZE, ROWS), jnp.bfloat16),
            pltpu.VMEM((ROWS, ROWS), jnp.float32),
            pltpu.VMEM((ROWS, ROWS), jnp.float32),
        ],
        compiler_params=pltpu.CompilerParams(vmem_limit_bytes=VMEM),
        name="attend",
    )(used, table, units)


def plan(clusters):
    plane = lax.axis_index("z")
    server = lax.axis_index(PLANE)
    clusters = jnp.pad(clusters.T, ((0, SLOT_HEADS - HEADS), (0, 0)))
    tiles = clusters.reshape(SLOT_HEADS, GROUPS, GROUP_TILES)
    index = jnp.arange(GROUP_TILES, dtype=jnp.int32)
    mine, other = tiles[:, :, :, None], tiles[:, :, None, :]
    ahead = (other < mine) | ((other == mine) & (index[None, :] < index[:, None]))
    place = jnp.sum(ahead, axis=3, dtype=jnp.int32)
    at_place = place[:, :, None, :] == index[:, None]
    unit_cluster = jnp.sum(
        jnp.where(at_place[:, :, ::MATCH], tiles[:, :, None, :], 0), axis=3
    ).reshape(SLOT_HEADS, -1)
    units = unit_cluster.shape[1]
    number = jnp.arange(units, dtype=jnp.int32)
    same = unit_cluster[:, :, None] == unit_cluster[:, None, :]
    size = jnp.sum(same, axis=2, dtype=jnp.int32)
    rank = jnp.sum(same & (number[None, :] < number[:, None]), axis=2, dtype=jnp.int32)
    real = jnp.arange(SLOT_HEADS)[:, None] < HEADS
    again_cut = size >= SPLIT_AGAIN
    cut = jnp.where(again_cut, size * 13 // 20, jnp.where(size >= SPLIT, size * 7 // 10, 0))
    last_cut = jnp.where(again_cut, size - 1, cut)
    lead = (rank == 0) & real
    number_of_tasks = 3 * UNITS

    def loads(keys, queries):
        load = (2 * keys + queries) * SCALE + queries
        return jnp.where(lead & (queries > 0), load, 0).reshape(PLANES, UNITS)

    tasks = jnp.concatenate(
        [loads(size, size - last_cut), loads(cut, cut), loads(last_cut, last_cut - cut)], axis=1
    )
    every = jnp.arange(number_of_tasks, dtype=jnp.int32)
    mine, other = tasks[:, :, None], tasks[:, None, :]
    order = jnp.sum(
        (other > mine) | ((other == mine) & (every[None, :] < every[:, None])),
        axis=2,
        dtype=jnp.int32,
    )
    sizes = jnp.sum(
        jnp.where(order[:, None, :] == every[:UNITS, None], tasks[:, None, :], 0), axis=2
    )
    count = jnp.max(jnp.sum(tasks > 0, axis=1, dtype=jnp.int32)).reshape(1)
    sizes = jnp.broadcast_to(
        sizes.T.astype(jnp.float32)[:, :, None], (UNITS, PLANES, 128)
    )
    key, load = assign(count, sizes)
    load = jnp.where(jnp.arange(128)[None, :] < SERVERS, load, 0.0).astype(jnp.int32)
    most = jnp.max(load // SCALE), jnp.max(load % SCALE)
    key = lax.dynamic_slice(key, (0, plane, 0), (UNITS, 1, 1)).reshape(UNITS).astype(jnp.int32)
    load = lax.dynamic_index_in_dim(load, plane, 0, keepdims=False)
    first = plane * PER_PLANE

    def own(array):
        return lax.dynamic_slice_in_dim(array, first, PER_PLANE, 0)

    own_order = lax.dynamic_index_in_dim(order, plane, 0, keepdims=False)
    own_order = own_order.reshape(3, PER_PLANE, 1, units)
    own_rank, own_cut, own_last_cut = own(rank), own(cut), own(last_cut)
    leader = own(same) & (own_rank == 0)[:, None, :]
    task = jnp.sum(jnp.where(leader, own_order, 0), axis=3).reshape(3, UNITS)
    code = jnp.sum(
        jnp.where(task[:, :, None] == every[:UNITS], key, 0), axis=2
    )
    own_rank, own_cut = own_rank.reshape(UNITS), own_cut.reshape(UNITS)
    own_last_cut = own_last_cut.reshape(UNITS)
    owner, before = code % 128, code // 128
    query_base = before % SCALE
    base = (before // SCALE - query_base) // 2
    own_count = jnp.clip(HEADS - first, 0, PER_PLANE) * units
    live = every[:UNITS] < own_count
    in_front = (own_rank < own_cut) & live
    in_second = (own_rank < own_last_cut) & (own_last_cut > own_cut) & live

    def of_task(first, second, last):
        return jnp.where(in_front, first, jnp.where(in_second, second, last))

    query_owner = of_task(owner[1], owner[2], owner[0])
    query_slot = own_rank + of_task(
        query_base[1], query_base[2] - own_cut, query_base[0] - own_last_cut
    )
    copied = jnp.concatenate([in_front, in_second])
    entries = every[: 2 * UNITS]
    earlier = jnp.sum(
        copied[None, :] & (entries[None, :] < entries[:, None]), axis=1, dtype=jnp.int32
    )
    again = jnp.sum(
        jnp.where(copied[None, :] & (earlier[None, :] == entries[:, None]), entries[None, :], 0),
        axis=1,
    )
    place = jnp.concatenate(
        [query_owner * SCALE + query_slot]
        + [owner[i] * SCALE + base[i] + own_rank for i in range(3)]
        + [again]
    )
    tile_of = own(
        jnp.sum(jnp.where(at_place, index, 0), axis=3, dtype=jnp.int32)
    ) + jnp.arange(GROUPS, dtype=jnp.int32)[:, None] * GROUP_TILES
    here = (
        ((query_owner == server) & live)[None, :]
        & (query_slot[None, :] == jnp.arange(SCALE, dtype=jnp.int32)[:, None])
    )
    table = of_task(base[1], base[2], base[0]) * SCALE + own_rank
    table = jnp.sum(jnp.where(here, table[None, :], 0), axis=1)
    mine = jnp.sum(jnp.where(jnp.arange(128) == server, load, 0))
    used = jnp.stack([mine % SCALE, (mine // SCALE - mine % SCALE) // 2])
    counts = jnp.stack([own_count, jnp.sum(copied, dtype=jnp.int32)])
    tile_of = tile_of * PER_PLANE + jnp.arange(PER_PLANE, dtype=jnp.int32)[:, None, None]
    return (counts, tile_of.reshape(-1), place, table, used), most


def exchange(caps, arrived, count, tiles, place, table, used):
    pieces = arrived.reshape(-1, PIECE, HEAD_SIZE)
    packed = pack(caps, count, tiles, place, pieces)
    packed = packed.reshape(SERVERS, -1, UNIT_PIECE, HEAD_SIZE)
    units = lax.all_to_all(packed, PLANE, split_axis=0, concat_axis=0, tiled=True)
    results = attend(caps, used, table, units)
    results = lax.all_to_all(results, PLANE, split_axis=0, concat_axis=0, tiled=True)
    results = results.reshape(SERVERS * caps[1] * MATCH, PIECE, HEAD_SIZE)
    return unpack(caps, count, tiles, place, results)


def on_device(queries, keys, values, tile_cluster):
    clusters = jnp.broadcast_to(tile_cluster.reshape(1, 1, HEADS), (TILES, 1, HEADS))
    clusters = lax.all_to_all(clusters, AXES, split_axis=0, concat_axis=0, tiled=True)
    clusters = clusters.reshape(TILES, HEADS)
    outgoing = spread(queries, keys, values)
    arrived = lax.all_to_all(outgoing, AXES, split_axis=0, concat_axis=0, tiled=True)
    tables, (most_slabs, most_queries) = plan(clusters)
    which = jnp.int32(len(CAPACITIES) - 1)
    for i in range(len(CAPACITIES) - 2, -1, -1):
        fits = (most_slabs <= CAPACITIES[i][0]) & (most_queries <= CAPACITIES[i][1])
        which = jnp.where(fits, i, which)
    back = lax.switch(which, [partial(exchange, caps) for caps in CAPACITIES], arrived, *tables)
    back = lax.all_to_all(back, AXES, split_axis=0, concat_axis=0, tiled=True)
    back = back.reshape(2, PLANES, SERVERS // 2, PER_PLANE, PIECE, HEAD_SIZE)
    back = back.transpose(1, 3, 0, 2, 4, 5).reshape(SLOT_HEADS, TILE, HEAD_SIZE)
    return back[:HEADS]


def solution(mesh):
    fine = Mesh(mesh.devices.reshape(SIZES), AXES)
    rows = ("ylo", "z", "yhi", "x", "core")
    return jax.shard_map(
        on_device,
        mesh=fine,
        in_specs=(
            P(None, rows, None),
            P(None, rows, None),
            P(None, rows, None),
            P(None, rows),
        ),
        out_specs=P(None, rows, None),
        check_vma=False,
    )
```

```python
from functools import partial

import jax
import jax.numpy as jnp
from jax import lax
from jax.experimental import pallas as pl
from jax.experimental.pallas import tpu as pltpu
from jax.sharding import Mesh
from jax.sharding import PartitionSpec as P

AXES = ("ylo", "z", "yhi", "x", "core")
PLANE = ("ylo", "yhi", "x", "core")
SIZES = (2, 8, 2, 4, 2)

HEADS = 20
PLANES = 8
PER_PLANE = 3
SLOT_HEADS = PLANES * PER_PLANE
SERVERS = 32
GROUPS = 16
GROUP_TILES = 16
TILES = 256
TILE = 128
MATCH = 4
UNITS = PER_PLANE * GROUPS * GROUP_TILES // MATCH
PIECE = TILE // SERVERS
HEAD_SIZE = 128
CAPACITIES = ((21, 7), (23, 7), (26, 8), (32, 11), (72, 24))
SPLIT = 7
SPLIT_AGAIN = 9
SCALE = 64
STEP = 8
ROWS = MATCH * TILE
UNIT_PIECE = MATCH * PIECE
NEGATIVE = -1e30
VMEM = 56 * 1024 * 1024


def assign_kernel(count_ref, size_ref, key_ref, load_ref):
    lane = lax.broadcasted_iota(jnp.int32, (PLANES, 128), 1)
    lane_number = lane.astype(jnp.float32)
    load_ref[...] = jnp.where(lane < SERVERS, 0.0, 65536.0)

    def step(i, carry):
        load = load_ref[...]
        key = jnp.min(load * 128.0 + lane_number, axis=1, keepdims=True)
        owner = key - jnp.floor(key * (1.0 / 128.0)) * 128.0
        load_ref[...] = load + jnp.where(lane_number == owner, size_ref[i], 0.0)
        key_ref[i] = jnp.broadcast_to(key, (PLANES, 128))
        return carry

    lax.fori_loop(0, count_ref[0], step, 0)


def assign(count, sizes):
    return pl.pallas_call(
        assign_kernel,
        in_specs=[
            pl.BlockSpec(memory_space=pltpu.SMEM),
            pl.BlockSpec(memory_space=pltpu.VMEM),
        ],
        out_specs=[pl.BlockSpec(memory_space=pltpu.VMEM)] * 2,
        out_shape=[
            jax.ShapeDtypeStruct((UNITS, PLANES, 128), jnp.float32),
            jax.ShapeDtypeStruct((PLANES, 128), jnp.float32),
        ],
        compiler_params=pltpu.CompilerParams(vmem_limit_bytes=VMEM),
        name="assign",
    )(count, sizes)


def slab(code, depth, start, width):
    owner = lax.shift_right_logical(code, SCALE.bit_length() - 1)
    return owner * depth + start + (code & (SCALE - 1)) * width


def move_units(steps, tile_ref, move):
    def some(i, carry):
        moves = []
        for k in range(STEP):
            unit = i * STEP + k
            moves += move(unit, [tile_ref[unit * MATCH + j] for j in range(MATCH)])
        pieces = [load() for load, _ in moves]
        for piece, (_, store) in zip(pieces, moves):
            store(piece)
        return carry

    lax.fori_loop(0, steps, some, 0)


def mover(in_ref, source, out_ref, target):
    def store(piece):
        out_ref[target] = piece

    return lambda: in_ref[source], store


def pack_kernel(caps, count_ref, tile_ref, place_ref, in_ref, out_ref):
    depth = caps[0]

    def first(unit, tiles):
        to_query = slab(place_ref[unit], depth, depth - 1, -1) * MATCH
        to_keys = slab(place_ref[UNITS + unit], depth, 0, 2) * MATCH
        return [
            mover(in_ref, tile * 3 + s, out_ref, slot + j)
            for j, tile in enumerate(tiles)
            for s, slot in enumerate((to_query, to_keys, to_keys + MATCH))
        ]

    move_units(lax.shift_right_logical(count_ref[0], STEP.bit_length() - 1), tile_ref, first)

    def again(i, carry):
        entry = place_ref[4 * UNITS + i]
        unit = jnp.where(entry >= UNITS, entry - UNITS, entry)
        also = slab(place_ref[2 * UNITS + entry], depth, 0, 2) * MATCH
        tiles = [tile_ref[unit * MATCH + j] for j in range(MATCH)]
        pieces = [in_ref[tile * 3 + s] for s in (1, 2) for tile in tiles]
        for k, piece in enumerate(pieces):
            out_ref[also + k] = piece
        return carry

    lax.fori_loop(0, count_ref[1], again, 0)


def pack(caps, count, tiles, place, arrived):
    smem = pl.BlockSpec(memory_space=pltpu.SMEM)
    vmem = pl.BlockSpec(memory_space=pltpu.VMEM)
    return pl.pallas_call(
        partial(pack_kernel, caps),
        in_specs=[smem, smem, smem, vmem],
        out_specs=vmem,
        out_shape=jax.ShapeDtypeStruct(
            (SERVERS * caps[0] * MATCH, PIECE, HEAD_SIZE), jnp.bfloat16
        ),
        compiler_params=pltpu.CompilerParams(vmem_limit_bytes=VMEM),
        name="pack_units",
    )(count, tiles, place, arrived)


def unpack_kernel(caps, count_ref, tile_ref, place_ref, in_ref, out_ref):
    out_ref = out_ref.reshape(TILES * PER_PLANE, PIECE, HEAD_SIZE)

    def back(unit, tiles):
        slot = slab(place_ref[unit], caps[1], 0, 1) * MATCH
        return [mover(in_ref, slot + j, out_ref, tile) for j, tile in enumerate(tiles)]

    move_units(lax.shift_right_logical(count_ref[0], STEP.bit_length() - 1), tile_ref, back)


def unpack(caps, count, tiles, place, results):
    smem = pl.BlockSpec(memory_space=pltpu.SMEM)
    vmem = pl.BlockSpec(memory_space=pltpu.VMEM)
    return pl.pallas_call(
        partial(unpack_kernel, caps),
        in_specs=[smem, smem, smem, vmem],
        out_specs=vmem,
        out_shape=jax.ShapeDtypeStruct((TILES, PER_PLANE, PIECE, HEAD_SIZE), jnp.bfloat16),
        compiler_params=pltpu.CompilerParams(vmem_limit_bytes=VMEM),
        name="unpack_units",
    )(count, tiles, place, results)


def spread_kernel(*refs):
    out_ref = refs[3]
    half = SERVERS // 2
    for s in range(3):
        for head in range(HEADS):
            plane, slot = divmod(head, PER_PLANE)
            for y in range(2):
                devices = pl.ds((y * PLANES + plane) * half, half)
                out_ref[devices, slot * 3 + s] = refs[s][head, y * half : (y + 1) * half]


def spread(queries, keys, values):
    vmem = pl.BlockSpec(memory_space=pltpu.VMEM)
    pieces = [a.reshape(HEADS, SERVERS, PIECE, HEAD_SIZE) for a in (queries, keys, values)]
    return pl.pallas_call(
        spread_kernel,
        in_specs=[vmem] * 3,
        out_specs=vmem,
        out_shape=jax.ShapeDtypeStruct((TILES, PER_PLANE * 3, PIECE, HEAD_SIZE), jnp.bfloat16),
        compiler_params=pltpu.CompilerParams(vmem_limit_bytes=VMEM),
        name="spread_rows",
    )(*pieces)


def row_key(shape, dim):
    row = lax.broadcasted_iota(jnp.int32, shape, dim)
    piece = row // UNIT_PIECE
    tile = lax.rem(row // PIECE, MATCH)
    return tile * TILE + piece * PIECE + lax.rem(row, PIECE)


def attend_kernel(
    caps, used_ref, table_ref, in_ref, out_ref, peak_ref, total_ref, sum_ref, turned_ref, *score_refs
):
    factor = HEAD_SIZE**-0.5 * 1.4426950408889634

    def rows(which):
        return in_ref[:, which].reshape(ROWS, HEAD_SIZE)

    def turn(unit, carry):
        turned_ref[unit] = rows(2 * unit + 1).T
        return carry

    lax.fori_loop(0, used_ref[1], turn, 0)

    def one_query_unit(slot, carry):
        code = table_ref[slot]
        first = lax.shift_right_logical(code, SCALE.bit_length() - 1)
        earlier = code & (SCALE - 1)
        last = first + earlier
        query = rows(caps[0] - 1 - slot)

        def scores_of(unit):
            return lax.dot_general(
                rows(2 * unit), query, (((1,), (1,)), ((), ())), preferred_element_type=jnp.float32
            )

        def unit_at(step):
            return jnp.where(step == 0, last, jnp.minimum(first + step - 1, last))

        def fold(step, now, ahead=True):
            if ahead:
                score_refs[1 - now][...] = scores_of(unit_at(step + 1))
            scores = score_refs[now][...]
            old = peak_ref[...]
            peak = jnp.maximum(old, jnp.max(scores, axis=0, keepdims=True))
            weights = jnp.exp2((scores - peak) * factor)
            keep = jnp.exp2((old - peak) * factor)
            peak_ref[...] = peak
            total_ref[...] = total_ref[...] * keep + jnp.sum(weights, axis=0, keepdims=True)
            sum_ref[...] = sum_ref[...] * keep + jnp.dot(
                turned_ref[unit_at(step)],
                weights.astype(jnp.bfloat16),
                preferred_element_type=jnp.float32,
            )

        visible = row_key((ROWS, 1), 0) <= row_key((1, ROWS), 1)
        score_refs[0][...] = jnp.where(visible, scores_of(last), NEGATIVE)
        peak_ref[...] = jnp.full(peak_ref.shape, NEGATIVE, jnp.float32)
        total_ref[...] = jnp.zeros(total_ref.shape, jnp.float32)
        sum_ref[...] = jnp.zeros(sum_ref.shape, jnp.float32)

        def two(i, carry):
            fold(2 * i, 0)
            fold(2 * i + 1, 1)
            return carry

        lax.fori_loop(0, lax.shift_right_logical(earlier + 1, 1), two, 0)

        @pl.when((earlier & 1) == 0)
        def _():
            fold(earlier, 0, ahead=False)

        result = (sum_ref[...] / total_ref[...]).T.astype(jnp.bfloat16)
        out_ref[:, slot] = result.reshape(SERVERS, UNIT_PIECE, HEAD_SIZE)
        return carry

    lax.fori_loop(0, used_ref[0], one_query_unit, 0)


def attend(caps, used, table, units):
    smem = pl.BlockSpec(memory_space=pltpu.SMEM)
    vmem = pl.BlockSpec(memory_space=pltpu.VMEM)
    return pl.pallas_call(
        partial(attend_kernel, caps),
        in_specs=[smem, smem, vmem],
        out_specs=vmem,
        out_shape=jax.ShapeDtypeStruct((SERVERS, caps[1], UNIT_PIECE, HEAD_SIZE), jnp.bfloat16),
        scratch_shapes=[
            pltpu.VMEM((1, ROWS), jnp.float32),
            pltpu.VMEM((1, ROWS), jnp.float32),
            pltpu.VMEM((HEAD_SIZE, ROWS), jnp.float32),
            pltpu.VMEM((caps[0] // 2, HEAD_SIZE, ROWS), jnp.bfloat16),
            pltpu.VMEM((ROWS, ROWS), jnp.float32),
            pltpu.VMEM((ROWS, ROWS), jnp.float32),
        ],
        compiler_params=pltpu.CompilerParams(vmem_limit_bytes=VMEM),
        name="attend",
    )(used, table, units)


def plan(clusters):
    plane = lax.axis_index("z")
    server = lax.axis_index(PLANE)
    clusters = jnp.pad(clusters.T, ((0, SLOT_HEADS - HEADS), (0, 0)))
    tiles = clusters.reshape(SLOT_HEADS, GROUPS, GROUP_TILES)
    index = jnp.arange(GROUP_TILES, dtype=jnp.int32)
    mine, other = tiles[:, :, :, None], tiles[:, :, None, :]
    ahead = (other < mine) | ((other == mine) & (index[None, :] < index[:, None]))
    place = jnp.sum(ahead, axis=3, dtype=jnp.int32)
    at_place = place[:, :, None, :] == index[:, None]
    unit_cluster = jnp.sum(
        jnp.where(at_place[:, :, ::MATCH], tiles[:, :, None, :], 0), axis=3
    ).reshape(SLOT_HEADS, -1)
    units = unit_cluster.shape[1]
    number = jnp.arange(units, dtype=jnp.int32)
    same = unit_cluster[:, :, None] == unit_cluster[:, None, :]
    size = jnp.sum(same, axis=2, dtype=jnp.int32)
    rank = jnp.sum(same & (number[None, :] < number[:, None]), axis=2, dtype=jnp.int32)
    real = jnp.arange(SLOT_HEADS)[:, None] < HEADS
    again_cut = size >= SPLIT_AGAIN
    cut = jnp.where(again_cut, size * 13 // 20, jnp.where(size >= SPLIT, size * 7 // 10, 0))
    last_cut = jnp.where(again_cut, size - 1, cut)
    lead = (rank == 0) & real
    number_of_tasks = 3 * UNITS

    def loads(keys, queries):
        load = (2 * keys + queries) * SCALE + queries
        return jnp.where(lead & (queries > 0), load, 0).reshape(PLANES, UNITS)

    tasks = jnp.concatenate(
        [loads(size, size - last_cut), loads(cut, cut), loads(last_cut, last_cut - cut)], axis=1
    )
    every = jnp.arange(number_of_tasks, dtype=jnp.int32)
    mine, other = tasks[:, :, None], tasks[:, None, :]
    order = jnp.sum(
        (other > mine) | ((other == mine) & (every[None, :] < every[:, None])),
        axis=2,
        dtype=jnp.int32,
    )
    sizes = jnp.sum(
        jnp.where(order[:, None, :] == every[:UNITS, None], tasks[:, None, :], 0), axis=2
    )
    count = jnp.max(jnp.sum(tasks > 0, axis=1, dtype=jnp.int32)).reshape(1)
    sizes = jnp.broadcast_to(
        sizes.T.astype(jnp.float32)[:, :, None], (UNITS, PLANES, 128)
    )
    key, load = assign(count, sizes)
    load = jnp.where(jnp.arange(128)[None, :] < SERVERS, load, 0.0).astype(jnp.int32)
    most = jnp.max(load // SCALE), jnp.max(load % SCALE)
    key = lax.dynamic_slice(key, (0, plane, 0), (UNITS, 1, 1)).reshape(UNITS).astype(jnp.int32)
    load = lax.dynamic_index_in_dim(load, plane, 0, keepdims=False)
    first = plane * PER_PLANE

    def own(array):
        return lax.dynamic_slice_in_dim(array, first, PER_PLANE, 0)

    own_order = lax.dynamic_index_in_dim(order, plane, 0, keepdims=False)
    own_order = own_order.reshape(3, PER_PLANE, 1, units)
    own_rank, own_cut, own_last_cut = own(rank), own(cut), own(last_cut)
    leader = own(same) & (own_rank == 0)[:, None, :]
    task = jnp.sum(jnp.where(leader, own_order, 0), axis=3).reshape(3, UNITS)
    code = jnp.sum(
        jnp.where(task[:, :, None] == every[:UNITS], key, 0), axis=2
    )
    own_rank, own_cut = own_rank.reshape(UNITS), own_cut.reshape(UNITS)
    own_last_cut = own_last_cut.reshape(UNITS)
    owner, before = code % 128, code // 128
    query_base = before % SCALE
    base = (before // SCALE - query_base) // 2
    own_count = jnp.clip(HEADS - first, 0, PER_PLANE) * units
    live = every[:UNITS] < own_count
    in_front = (own_rank < own_cut) & live
    in_second = (own_rank < own_last_cut) & (own_last_cut > own_cut) & live

    def of_task(first, second, last):
        return jnp.where(in_front, first, jnp.where(in_second, second, last))

    query_owner = of_task(owner[1], owner[2], owner[0])
    query_slot = own_rank + of_task(
        query_base[1], query_base[2] - own_cut, query_base[0] - own_last_cut
    )
    copied = jnp.concatenate([in_front, in_second])
    entries = every[: 2 * UNITS]
    earlier = jnp.sum(
        copied[None, :] & (entries[None, :] < entries[:, None]), axis=1, dtype=jnp.int32
    )
    again = jnp.sum(
        jnp.where(copied[None, :] & (earlier[None, :] == entries[:, None]), entries[None, :], 0),
        axis=1,
    )
    place = jnp.concatenate(
        [query_owner * SCALE + query_slot]
        + [owner[i] * SCALE + base[i] + own_rank for i in range(3)]
        + [again]
    )
    tile_of = own(
        jnp.sum(jnp.where(at_place, index, 0), axis=3, dtype=jnp.int32)
    ) + jnp.arange(GROUPS, dtype=jnp.int32)[:, None] * GROUP_TILES
    here = (
        ((query_owner == server) & live)[None, :]
        & (query_slot[None, :] == jnp.arange(SCALE, dtype=jnp.int32)[:, None])
    )
    table = of_task(base[1], base[2], base[0]) * SCALE + own_rank
    table = jnp.sum(jnp.where(here, table[None, :], 0), axis=1)
    mine = jnp.sum(jnp.where(jnp.arange(128) == server, load, 0))
    used = jnp.stack([mine % SCALE, (mine // SCALE - mine % SCALE) // 2])
    counts = jnp.stack([own_count, jnp.sum(copied, dtype=jnp.int32)])
    tile_of = tile_of * PER_PLANE + jnp.arange(PER_PLANE, dtype=jnp.int32)[:, None, None]
    return (counts, tile_of.reshape(-1), place, table, used), most


def exchange(caps, arrived, count, tiles, place, table, used):
    pieces = arrived.reshape(-1, PIECE, HEAD_SIZE)
    packed = pack(caps, count, tiles, place, pieces)
    packed = packed.reshape(SERVERS, -1, UNIT_PIECE, HEAD_SIZE)
    units = lax.all_to_all(packed, PLANE, split_axis=0, concat_axis=0, tiled=True)
    results = attend(caps, used, table, units)
    results = lax.all_to_all(results, PLANE, split_axis=0, concat_axis=0, tiled=True)
    results = results.reshape(SERVERS * caps[1] * MATCH, PIECE, HEAD_SIZE)
    return unpack(caps, count, tiles, place, results)


def on_device(queries, keys, values, tile_cluster):
    clusters = jnp.broadcast_to(tile_cluster.reshape(1, 1, HEADS), (TILES, 1, HEADS))
    clusters = lax.all_to_all(clusters, AXES, split_axis=0, concat_axis=0, tiled=True)
    clusters = clusters.reshape(TILES, HEADS)
    outgoing = spread(queries, keys, values)
    arrived = lax.all_to_all(outgoing, AXES, split_axis=0, concat_axis=0, tiled=True)
    tables, (most_slabs, most_queries) = plan(clusters)
    which = jnp.int32(len(CAPACITIES) - 1)
    for i in range(len(CAPACITIES) - 2, -1, -1):
        fits = (most_slabs <= CAPACITIES[i][0]) & (most_queries <= CAPACITIES[i][1])
        which = jnp.where(fits, i, which)
    back = lax.switch(which, [partial(exchange, caps) for caps in CAPACITIES], arrived, *tables)
    back = lax.all_to_all(back, AXES, split_axis=0, concat_axis=0, tiled=True)
    back = back.reshape(2, PLANES, SERVERS // 2, PER_PLANE, PIECE, HEAD_SIZE)
    back = back.transpose(1, 3, 0, 2, 4, 5).reshape(SLOT_HEADS, TILE, HEAD_SIZE)
    return back[:HEADS]


def solution(mesh):
    fine = Mesh(mesh.devices.reshape(SIZES), AXES)
    rows = ("ylo", "z", "yhi", "x", "core")
    return jax.shard_map(
        on_device,
        mesh=fine,
        in_specs=(
            P(None, rows, None),
            P(None, rows, None),
            P(None, rows, None),
            P(None, rows),
        ),
        out_specs=P(None, rows, None),
        check_vma=False,
    )
```

```python
from functools import partial

import jax
import jax.numpy as jnp
from jax import lax
from jax.experimental import pallas as pl
from jax.experimental.pallas import tpu as pltpu
from jax.sharding import Mesh
from jax.sharding import PartitionSpec as P

AXES = ("ylo", "z", "yhi", "x", "core")
PLANE = ("ylo", "yhi", "x", "core")
SIZES = (2, 8, 2, 4, 2)

HEADS = 20
PLANES = 8
PER_PLANE = 3
SLOT_HEADS = PLANES * PER_PLANE
SERVERS = 32
GROUPS = 16
GROUP_TILES = 16
TILES = 256
TILE = 128
MATCH = 4
UNITS = PER_PLANE * GROUPS * GROUP_TILES // MATCH
PIECE = TILE // SERVERS
HEAD_SIZE = 128
CAPACITIES = ((21, 7), (23, 7), (26, 8), (32, 11), (72, 24))
SPLIT = 7
SPLIT_AGAIN = 9
SCALE = 64
STEP = 16
ROWS = MATCH * TILE
UNIT_PIECE = MATCH * PIECE
NEGATIVE = -1e30
VMEM = 56 * 1024 * 1024


def assign_kernel(count_ref, size_ref, key_ref, load_ref):
    lane = lax.broadcasted_iota(jnp.int32, (PLANES, 128), 1)
    lane_number = lane.astype(jnp.float32)
    load_ref[...] = jnp.where(lane < SERVERS, 0.0, 65536.0)

    def step(i, carry):
        load = load_ref[...]
        key = jnp.min(load * 128.0 + lane_number, axis=1, keepdims=True)
        owner = key - jnp.floor(key * (1.0 / 128.0)) * 128.0
        load_ref[...] = load + jnp.where(lane_number == owner, size_ref[i], 0.0)
        key_ref[i] = jnp.broadcast_to(key, (PLANES, 128))
        return carry

    lax.fori_loop(0, count_ref[0], step, 0)


def assign(count, sizes):
    return pl.pallas_call(
        assign_kernel,
        in_specs=[
            pl.BlockSpec(memory_space=pltpu.SMEM),
            pl.BlockSpec(memory_space=pltpu.VMEM),
        ],
        out_specs=[pl.BlockSpec(memory_space=pltpu.VMEM)] * 2,
        out_shape=[
            jax.ShapeDtypeStruct((UNITS, PLANES, 128), jnp.float32),
            jax.ShapeDtypeStruct((PLANES, 128), jnp.float32),
        ],
        compiler_params=pltpu.CompilerParams(vmem_limit_bytes=VMEM),
        name="assign",
    )(count, sizes)


def slab(code, depth, start, width):
    owner = lax.shift_right_logical(code, SCALE.bit_length() - 1)
    return owner * depth + start + (code & (SCALE - 1)) * width


def move_units(steps, tile_ref, move):
    def some(i, carry):
        moves = []
        for k in range(STEP):
            unit = i * STEP + k
            moves += move(unit, [tile_ref[unit * MATCH + j] for j in range(MATCH)])
        pieces = [load() for load, _ in moves]
        for piece, (_, store) in zip(pieces, moves):
            store(piece)
        return carry

    lax.fori_loop(0, steps, some, 0)


def mover(in_ref, source, out_ref, target):
    def store(piece):
        out_ref[target] = piece

    return lambda: in_ref[source], store


def pack_kernel(caps, count_ref, tile_ref, place_ref, in_ref, out_ref):
    depth = caps[0]

    def first(unit, tiles):
        to_query = slab(place_ref[unit], depth, depth - 1, -1) * MATCH
        to_keys = slab(place_ref[UNITS + unit], depth, 0, 2) * MATCH
        return [
            mover(in_ref, tile * 3 + s, out_ref, slot + j)
            for j, tile in enumerate(tiles)
            for s, slot in enumerate((to_query, to_keys, to_keys + MATCH))
        ]

    move_units(lax.shift_right_logical(count_ref[0], STEP.bit_length() - 1), tile_ref, first)

    def again(i, carry):
        entry = place_ref[4 * UNITS + i]
        unit = jnp.where(entry >= UNITS, entry - UNITS, entry)
        also = slab(place_ref[2 * UNITS + entry], depth, 0, 2) * MATCH
        tiles = [tile_ref[unit * MATCH + j] for j in range(MATCH)]
        pieces = [in_ref[tile * 3 + s] for s in (1, 2) for tile in tiles]
        for k, piece in enumerate(pieces):
            out_ref[also + k] = piece
        return carry

    lax.fori_loop(0, count_ref[1], again, 0)


def pack(caps, count, tiles, place, arrived):
    smem = pl.BlockSpec(memory_space=pltpu.SMEM)
    vmem = pl.BlockSpec(memory_space=pltpu.VMEM)
    return pl.pallas_call(
        partial(pack_kernel, caps),
        in_specs=[smem, smem, smem, vmem],
        out_specs=vmem,
        out_shape=jax.ShapeDtypeStruct(
            (SERVERS * caps[0] * MATCH, PIECE, HEAD_SIZE), jnp.bfloat16
        ),
        compiler_params=pltpu.CompilerParams(vmem_limit_bytes=VMEM),
        name="pack_units",
    )(count, tiles, place, arrived)


def unpack_kernel(caps, count_ref, tile_ref, place_ref, in_ref, out_ref):
    out_ref = out_ref.reshape(TILES * PER_PLANE, PIECE, HEAD_SIZE)

    def back(unit, tiles):
        slot = slab(place_ref[unit], caps[1], 0, 1) * MATCH
        return [mover(in_ref, slot + j, out_ref, tile) for j, tile in enumerate(tiles)]

    move_units(lax.shift_right_logical(count_ref[0], STEP.bit_length() - 1), tile_ref, back)


def unpack(caps, count, tiles, place, results):
    smem = pl.BlockSpec(memory_space=pltpu.SMEM)
    vmem = pl.BlockSpec(memory_space=pltpu.VMEM)
    return pl.pallas_call(
        partial(unpack_kernel, caps),
        in_specs=[smem, smem, smem, vmem],
        out_specs=vmem,
        out_shape=jax.ShapeDtypeStruct((TILES, PER_PLANE, PIECE, HEAD_SIZE), jnp.bfloat16),
        compiler_params=pltpu.CompilerParams(vmem_limit_bytes=VMEM),
        name="unpack_units",
    )(count, tiles, place, results)


def spread_kernel(*refs):
    out_ref = refs[3]
    half = SERVERS // 2
    for s in range(3):
        for head in range(HEADS):
            plane, slot = divmod(head, PER_PLANE)
            for y in range(2):
                devices = pl.ds((y * PLANES + plane) * half, half)
                out_ref[devices, slot * 3 + s] = refs[s][head, y * half : (y + 1) * half]


def spread(queries, keys, values):
    vmem = pl.BlockSpec(memory_space=pltpu.VMEM)
    pieces = [a.reshape(HEADS, SERVERS, PIECE, HEAD_SIZE) for a in (queries, keys, values)]
    return pl.pallas_call(
        spread_kernel,
        in_specs=[vmem] * 3,
        out_specs=vmem,
        out_shape=jax.ShapeDtypeStruct((TILES, PER_PLANE * 3, PIECE, HEAD_SIZE), jnp.bfloat16),
        compiler_params=pltpu.CompilerParams(vmem_limit_bytes=VMEM),
        name="spread_rows",
    )(*pieces)


def row_key(shape, dim):
    row = lax.broadcasted_iota(jnp.int32, shape, dim)
    piece = row // UNIT_PIECE
    tile = lax.rem(row // PIECE, MATCH)
    return tile * TILE + piece * PIECE + lax.rem(row, PIECE)


def attend_kernel(
    caps, used_ref, table_ref, in_ref, out_ref, peak_ref, total_ref, sum_ref, turned_ref, *score_refs
):
    factor = HEAD_SIZE**-0.5 * 1.4426950408889634

    def rows(which):
        return in_ref[:, which].reshape(ROWS, HEAD_SIZE)

    def turn(unit, carry):
        turned_ref[unit] = rows(2 * unit + 1).T
        return carry

    lax.fori_loop(0, used_ref[1], turn, 0)

    def one_query_unit(slot, carry):
        code = table_ref[slot]
        first = lax.shift_right_logical(code, SCALE.bit_length() - 1)
        earlier = code & (SCALE - 1)
        last = first + earlier
        query = rows(caps[0] - 1 - slot)

        def scores_of(unit):
            return lax.dot_general(
                rows(2 * unit), query, (((1,), (1,)), ((), ())), preferred_element_type=jnp.float32
            )

        def unit_at(step):
            return jnp.where(step == 0, last, jnp.minimum(first + step - 1, last))

        def fold(step, now):
            score_refs[1 - now][...] = scores_of(unit_at(step + 1))
            scores = score_refs[now][...]
            old = peak_ref[...]
            peak = jnp.maximum(old, jnp.max(scores, axis=0, keepdims=True))
            weights = jnp.exp2((scores - peak) * factor)
            keep = jnp.exp2((old - peak) * factor)
            peak_ref[...] = peak
            total_ref[...] = total_ref[...] * keep + jnp.sum(weights, axis=0, keepdims=True)
            sum_ref[...] = sum_ref[...] * keep + jnp.dot(
                turned_ref[unit_at(step)],
                weights.astype(jnp.bfloat16),
                preferred_element_type=jnp.float32,
            )

        visible = row_key((ROWS, 1), 0) <= row_key((1, ROWS), 1)
        score_refs[0][...] = jnp.where(visible, scores_of(last), NEGATIVE)
        peak_ref[...] = jnp.full(peak_ref.shape, NEGATIVE, jnp.float32)
        total_ref[...] = jnp.zeros(total_ref.shape, jnp.float32)
        sum_ref[...] = jnp.zeros(sum_ref.shape, jnp.float32)

        def two(i, carry):
            fold(2 * i, 0)
            fold(2 * i + 1, 1)
            return carry

        lax.fori_loop(0, lax.shift_right_logical(earlier + 1, 1), two, 0)

        @pl.when((earlier & 1) == 0)
        def _():
            fold(earlier, 0)

        result = (sum_ref[...] / total_ref[...]).T.astype(jnp.bfloat16)
        out_ref[:, slot] = result.reshape(SERVERS, UNIT_PIECE, HEAD_SIZE)
        return carry

    lax.fori_loop(0, used_ref[0], one_query_unit, 0)


def attend(caps, used, table, units):
    smem = pl.BlockSpec(memory_space=pltpu.SMEM)
    vmem = pl.BlockSpec(memory_space=pltpu.VMEM)
    return pl.pallas_call(
        partial(attend_kernel, caps),
        in_specs=[smem, smem, vmem],
        out_specs=vmem,
        out_shape=jax.ShapeDtypeStruct((SERVERS, caps[1], UNIT_PIECE, HEAD_SIZE), jnp.bfloat16),
        scratch_shapes=[
            pltpu.VMEM((1, ROWS), jnp.float32),
            pltpu.VMEM((1, ROWS), jnp.float32),
            pltpu.VMEM((HEAD_SIZE, ROWS), jnp.float32),
            pltpu.VMEM((caps[0] // 2, HEAD_SIZE, ROWS), jnp.bfloat16),
            pltpu.VMEM((ROWS, ROWS), jnp.float32),
            pltpu.VMEM((ROWS, ROWS), jnp.float32),
        ],
        compiler_params=pltpu.CompilerParams(vmem_limit_bytes=VMEM),
        name="attend",
    )(used, table, units)


def plan(clusters):
    plane = lax.axis_index("z")
    server = lax.axis_index(PLANE)
    clusters = jnp.pad(clusters.T, ((0, SLOT_HEADS - HEADS), (0, 0)))
    tiles = clusters.reshape(SLOT_HEADS, GROUPS, GROUP_TILES)
    index = jnp.arange(GROUP_TILES, dtype=jnp.int32)
    mine, other = tiles[:, :, :, None], tiles[:, :, None, :]
    ahead = (other < mine) | ((other == mine) & (index[None, :] < index[:, None]))
    place = jnp.sum(ahead, axis=3, dtype=jnp.int32)
    at_place = place[:, :, None, :] == index[:, None]
    unit_cluster = jnp.sum(
        jnp.where(at_place[:, :, ::MATCH], tiles[:, :, None, :], 0), axis=3
    ).reshape(SLOT_HEADS, -1)
    units = unit_cluster.shape[1]
    number = jnp.arange(units, dtype=jnp.int32)
    same = unit_cluster[:, :, None] == unit_cluster[:, None, :]
    size = jnp.sum(same, axis=2, dtype=jnp.int32)
    rank = jnp.sum(same & (number[None, :] < number[:, None]), axis=2, dtype=jnp.int32)
    real = jnp.arange(SLOT_HEADS)[:, None] < HEADS
    again_cut = size >= SPLIT_AGAIN
    cut = jnp.where(again_cut, size * 13 // 20, jnp.where(size >= SPLIT, size * 7 // 10, 0))
    last_cut = jnp.where(again_cut, size - 1, cut)
    lead = (rank == 0) & real
    number_of_tasks = 3 * UNITS

    def loads(keys, queries):
        load = (2 * keys + queries) * SCALE + queries
        return jnp.where(lead & (queries > 0), load, 0).reshape(PLANES, UNITS)

    tasks = jnp.concatenate(
        [loads(size, size - last_cut), loads(cut, cut), loads(last_cut, last_cut - cut)], axis=1
    )
    every = jnp.arange(number_of_tasks, dtype=jnp.int32)
    mine, other = tasks[:, :, None], tasks[:, None, :]
    order = jnp.sum(
        (other > mine) | ((other == mine) & (every[None, :] < every[:, None])),
        axis=2,
        dtype=jnp.int32,
    )
    sizes = jnp.sum(
        jnp.where(order[:, None, :] == every[:UNITS, None], tasks[:, None, :], 0), axis=2
    )
    count = jnp.max(jnp.sum(tasks > 0, axis=1, dtype=jnp.int32)).reshape(1)
    sizes = jnp.broadcast_to(
        sizes.T.astype(jnp.float32)[:, :, None], (UNITS, PLANES, 128)
    )
    key, load = assign(count, sizes)
    load = jnp.where(jnp.arange(128)[None, :] < SERVERS, load, 0.0).astype(jnp.int32)
    most = jnp.max(load // SCALE), jnp.max(load % SCALE)
    key = lax.dynamic_slice(key, (0, plane, 0), (UNITS, 1, 1)).reshape(UNITS).astype(jnp.int32)
    load = lax.dynamic_index_in_dim(load, plane, 0, keepdims=False)
    first = plane * PER_PLANE

    def own(array):
        return lax.dynamic_slice_in_dim(array, first, PER_PLANE, 0)

    own_order = lax.dynamic_index_in_dim(order, plane, 0, keepdims=False)
    own_order = own_order.reshape(3, PER_PLANE, 1, units)
    own_rank, own_cut, own_last_cut = own(rank), own(cut), own(last_cut)
    leader = own(same) & (own_rank == 0)[:, None, :]
    task = jnp.sum(jnp.where(leader, own_order, 0), axis=3).reshape(3, UNITS)
    code = jnp.sum(
        jnp.where(task[:, :, None] == every[:UNITS], key, 0), axis=2
    )
    own_rank, own_cut = own_rank.reshape(UNITS), own_cut.reshape(UNITS)
    own_last_cut = own_last_cut.reshape(UNITS)
    owner, before = code % 128, code // 128
    query_base = before % SCALE
    base = (before // SCALE - query_base) // 2
    own_count = jnp.clip(HEADS - first, 0, PER_PLANE) * units
    live = every[:UNITS] < own_count
    in_front = (own_rank < own_cut) & live
    in_second = (own_rank < own_last_cut) & (own_last_cut > own_cut) & live

    def of_task(first, second, last):
        return jnp.where(in_front, first, jnp.where(in_second, second, last))

    query_owner = of_task(owner[1], owner[2], owner[0])
    query_slot = own_rank + of_task(
        query_base[1], query_base[2] - own_cut, query_base[0] - own_last_cut
    )
    copied = jnp.concatenate([in_front, in_second])
    entries = every[: 2 * UNITS]
    earlier = jnp.sum(
        copied[None, :] & (entries[None, :] < entries[:, None]), axis=1, dtype=jnp.int32
    )
    again = jnp.sum(
        jnp.where(copied[None, :] & (earlier[None, :] == entries[:, None]), entries[None, :], 0),
        axis=1,
    )
    place = jnp.concatenate(
        [query_owner * SCALE + query_slot]
        + [owner[i] * SCALE + base[i] + own_rank for i in range(3)]
        + [again]
    )
    tile_of = own(
        jnp.sum(jnp.where(at_place, index, 0), axis=3, dtype=jnp.int32)
    ) + jnp.arange(GROUPS, dtype=jnp.int32)[:, None] * GROUP_TILES
    here = (
        ((query_owner == server) & live)[None, :]
        & (query_slot[None, :] == jnp.arange(SCALE, dtype=jnp.int32)[:, None])
    )
    table = of_task(base[1], base[2], base[0]) * SCALE + own_rank
    table = jnp.sum(jnp.where(here, table[None, :], 0), axis=1)
    mine = jnp.sum(jnp.where(jnp.arange(128) == server, load, 0))
    used = jnp.stack([mine % SCALE, (mine // SCALE - mine % SCALE) // 2])
    counts = jnp.stack([own_count, jnp.sum(copied, dtype=jnp.int32)])
    tile_of = tile_of * PER_PLANE + jnp.arange(PER_PLANE, dtype=jnp.int32)[:, None, None]
    return (counts, tile_of.reshape(-1), place, table, used), most


def exchange(caps, arrived, count, tiles, place, table, used):
    pieces = arrived.reshape(-1, PIECE, HEAD_SIZE)
    packed = pack(caps, count, tiles, place, pieces)
    packed = packed.reshape(SERVERS, -1, UNIT_PIECE, HEAD_SIZE)
    units = lax.all_to_all(packed, PLANE, split_axis=0, concat_axis=0, tiled=True)
    results = attend(caps, used, table, units)
    results = lax.all_to_all(results, PLANE, split_axis=0, concat_axis=0, tiled=True)
    results = results.reshape(SERVERS * caps[1] * MATCH, PIECE, HEAD_SIZE)
    return unpack(caps, count, tiles, place, results)


def on_device(queries, keys, values, tile_cluster):
    clusters = jnp.broadcast_to(tile_cluster.reshape(1, 1, HEADS), (TILES, 1, HEADS))
    clusters = lax.all_to_all(clusters, AXES, split_axis=0, concat_axis=0, tiled=True)
    clusters = clusters.reshape(TILES, HEADS)
    outgoing = spread(queries, keys, values)
    arrived = lax.all_to_all(outgoing, AXES, split_axis=0, concat_axis=0, tiled=True)
    tables, (most_slabs, most_queries) = plan(clusters)
    which = jnp.int32(len(CAPACITIES) - 1)
    for i in range(len(CAPACITIES) - 2, -1, -1):
        fits = (most_slabs <= CAPACITIES[i][0]) & (most_queries <= CAPACITIES[i][1])
        which = jnp.where(fits, i, which)
    back = lax.switch(which, [partial(exchange, caps) for caps in CAPACITIES], arrived, *tables)
    back = lax.all_to_all(back, AXES, split_axis=0, concat_axis=0, tiled=True)
    back = back.reshape(2, PLANES, SERVERS // 2, PER_PLANE, PIECE, HEAD_SIZE)
    back = back.transpose(1, 3, 0, 2, 4, 5).reshape(SLOT_HEADS, TILE, HEAD_SIZE)
    return back[:HEADS]


def solution(mesh):
    fine = Mesh(mesh.devices.reshape(SIZES), AXES)
    rows = ("ylo", "z", "yhi", "x", "core")
    return jax.shard_map(
        on_device,
        mesh=fine,
        in_specs=(
            P(None, rows, None),
            P(None, rows, None),
            P(None, rows, None),
            P(None, rows),
        ),
        out_specs=P(None, rows, None),
        check_vma=False,
    )
```
